32 devices in a mesh: dp: 8 (over z, x), rep: 4 (over y, core).
Axes of the slice: x: 2, y: 2, z: 4, core: 2. Of those that a mesh axis runs over, the one named last changes fastest.
Arguments:
- frames: bfloat16 [32, 3, 64, 2000], P(('dp', 'rep')), may hold values from -6 to 6
- weights: bfloat16 [2, 2000, 2000], replicated, may hold values from -0.125 to 0.125
- norm_gain: float32 [2, 2000], replicated, may hold values from 0.25 to 0.75
- norm_shift: float32 [2, 2000], replicated, may hold values from -0.2 to 0.2
- decays: float32 [2, 2000], replicated, may hold values from 0.85 to 0.99
- lengths: int32 [32], P(('dp', 'rep')), may hold values from 1 to 64, as said below
- cotangent: bfloat16 [32, 3, 64, 2000], P(('dp', 'rep')), may hold values from -6 to 6
Outputs:
- output: bfloat16 [32, 3, 64, 2000], P(('dp', 'rep'))
- grad_frames: bfloat16 [32, 3, 64, 2000], P(('dp', 'rep'))
- grad_weights: float32 [2, 2000, 2000], replicated
- grad_gain: float32 [2, 2000], replicated
- grad_shift: float32 [2, 2000], replicated
- grad_decay: float32 [2, 2000], replicated
The draws below stay inside these ranges and needn't reach their ends.
Inputs may be any that keep to these rules, and one draw needn't show every extreme that they name: `lengths`: each group's number of valid frames, a prefix of its slots; some group has exactly 64.
All inputs are finite; a program needn't handle non-finite values.
Results may differ from the reference program's by a relative error of at most 0.0046.
Values sent between devices are 32-bit elements; how exact they have to be, the bound alone decides.
A program may use at most 256 MiB of HBM per device.

```python
import jax
import jax.numpy as jnp
from jax import lax

H = 2000
VIEWS = 3
LAYERS = 2
LEN = 64
GROUPS = 32


def draw_lengths(key, part):
    key = jax.random.fold_in(key, 7)
    first_key, second_key = jax.random.split(key)
    shortest = max(1, LEN // 3)
    drawn = jax.random.randint(first_key, (GROUPS,), shortest, LEN + 1)
    chosen = jax.random.randint(second_key, (), 0, GROUPS)
    drawn = jnp.where(jnp.arange(GROUPS) == chosen, LEN, drawn)
    return drawn.astype(jnp.int32)


def block_levels(rng, dims, cuts, smallest, high):
    loudness = 1.0
    for axis_at, blocks in cuts:
        heights = jax.random.uniform(jax.random.fold_in(jax.random.fold_in(rng, 6), axis_at), (blocks,), jnp.float32, smallest / len(cuts), high / len(cuts))
        loudness = loudness * jnp.repeat(jnp.exp(heights), dims[axis_at] // blocks).reshape((-1,) + (1,) * (len(dims) - 1 - axis_at))
    return loudness


def normal_values(stream_key, extent, deviation, most, shards=(), kind=jnp.bfloat16):
    values = jax.random.normal(stream_key, extent, jnp.float32) * deviation
    if len(shards) > 0:
        values = block_levels(stream_key, extent, shards, -0.22, 0.18) * values
    return jnp.clip(values, min=-most, max=most).astype(kind)


def setup_inputs(seed: int = 0) -> dict:
    arg_keys = jax.random.split(jax.random.key(seed), 8)
    frames = normal_values(arg_keys[0], (GROUPS, VIEWS, LEN, H), 1.0, 6.0, ((0, 32),))
    weights = normal_values(arg_keys[1], (LAYERS, H, H), H ** -0.5, 0.125)
    norm_gain = jnp.clip(jax.random.uniform(arg_keys[2], (LAYERS, H), jnp.float32, 0.25, 0.75), 0.25, 0.75)
    norm_shift = normal_values(arg_keys[3], (LAYERS, H), 0.05, 0.2, (), jnp.float32)
    decays = jnp.clip(jax.random.uniform(arg_keys[4], (LAYERS, H), jnp.float32, 0.85, 0.99), 0.85, 0.99)
    lengths = draw_lengths(jax.random.fold_in(arg_keys[7], 71), 0)
    cotangent = normal_values(arg_keys[6], (GROUPS, VIEWS, LEN, H), 1.0, 6.0, ((0, 32),))
    return {"frames": frames, "weights": weights, "norm_gain": norm_gain, "norm_shift": norm_shift, "decays": decays, "lengths": lengths, "cotangent": cotangent}


eps = 1e-05

@jax.custom_vjp
def low(v):
    return lax.optimization_barrier(v.astype(jnp.bfloat16)).astype(jnp.float32)

@jax.custom_vjp
def low_back(v):
    return v

def low_keep(v):
    return (low(v), None)

def low_pass(kept, grad):
    return (grad,)

def back_keep(v):
    return (v, None)

def back_low(kept, grad):
    return (low(grad),)
low.defvjp(low_keep, low_pass)
low_back.defvjp(back_keep, back_low)

def recurrence(inputs, decay_rate):

    @jax.checkpoint
    def advance(carried, current):
        updated = decay_rate * carried + current
        return (updated, updated)
    series = jnp.moveaxis(inputs, 2, 0)
    start_state = jnp.zeros(series.shape[1:], jnp.float32)
    final_state, states = lax.scan(advance, start_state, series)
    return jnp.moveaxis(states, 0, 2)

def residual_layer(layer_in, weight, norm_gain, norm_shift, decay_rate, valid):
    rounded = low(layer_in)
    flat = rounded.reshape(-1, rounded.shape[-1])
    projected = jnp.dot(flat, weight, precision=lax.Precision.HIGHEST).reshape(layer_in.shape)
    projected = low_back(projected)
    total = jnp.sum(valid)
    average = lax.optimization_barrier(jnp.sum(valid * projected, axis=(0, 1, 2))) / total
    variance = lax.optimization_barrier(jnp.sum(valid * projected * projected, axis=(0, 1, 2))) / total - average * average
    normed = (projected - average) * lax.rsqrt(variance + eps)
    states = recurrence(norm_gain * normed + norm_shift, decay_rate)
    return layer_in + valid * jax.nn.softplus(states)

def reference(frames, weights, norm_gain, norm_shift, decays, lengths, cotangent):
    positions = jnp.arange(LEN, dtype=jnp.int32)
    valid = (positions[None, :] < lengths[:, None]).astype(jnp.float32)
    valid = jnp.broadcast_to(valid[:, None, :, None], (GROUPS, VIEWS, LEN, 1))

    def forward(inputs, weight_all, gain_all, shift_all, decay_all):
        middle = residual_layer(inputs, weight_all[0], gain_all[0], shift_all[0], decay_all[0], valid)
        return residual_layer(middle, weight_all[1], gain_all[1], shift_all[1], decay_all[1], valid)
    inputs = frames.astype(jnp.float32)
    weight_all = weights.astype(jnp.float32)
    result, pullback = jax.vjp(forward, inputs, weight_all, norm_gain, norm_shift, decays)
    grad_in, grad_weight, grad_gain, grad_shift, grad_decay = pullback(cotangent.astype(jnp.float32))
    return (result.astype(jnp.bfloat16), grad_in.astype(jnp.bfloat16), grad_weight, grad_gain, grad_shift, grad_decay)
```

```python
import functools

import jax
import jax.numpy as jnp
from jax import lax
from jax.experimental import pallas as pl
from jax.experimental.pallas import tpu as pltpu
from jax.sharding import PartitionSpec as P

EPS = 1e-05
MESH = pl.DeviceIdType.MESH
F32 = jnp.float32
BF16 = jnp.bfloat16
LANES = 128


def round_up(value, unit):
    return -(-value // unit) * unit


def pick_chunks(hidden, ring):
    best = None
    for chunks in (3, 4, 2, 1):
        shard = round_up(-(-hidden // ring), 8 * chunks)
        if best is None or shard * ring < best[0]:
            best = (shard * ring, chunks, shard // chunks)
    return best


def kernel(
    dims,
    frames,
    weights,
    gain,
    shift,
    decay,
    lengths,
    cotangent,
    output,
    grad_frames,
    grad_weights,
    grad_gain,
    grad_shift,
    grad_decay,
    wbuf,
    x0f,
    x1,
    x1r,
    xb,
    normed,
    states,
    gy,
    gpf,
    gpb,
    xr,
    gr,
    xchunk,
    gb,
    dw,
    ro,
    ra,
    params,
    coef,
    eight_f,
    eight_b,
    ring_f,
    ring_b,
    total_f,
    total_b,
    sem_w,
    sem_x,
    sem_g,
    sem_e,
    sem_r,
    sem_ro,
    sem_ra,
    sem_aa,
    sem_ag,
    sem_l,
):
    ring, chunks, chunk_rows, views, slots, hidden, width = dims
    rows = views * slots
    quarter = width // 4
    half = quarter // 2
    padded = ring * chunks * chunk_rows
    blocks = slots // 8
    lane_steps = width // LANES

    dp, rep = lax.axis_index("dp"), lax.axis_index("rep")
    a, bx = dp // 2, dp % 2
    by, c = rep // 2, rep % 2
    nx, ny, nc = 1 - bx, 1 - by, 1 - c

    def device(a_at, x_at, y_at, c_at):
        return (a_at * 2 + x_at, y_at * 2 + c_at)

    core_peer = device(a, bx, by, nc)
    x_peer = device(a, nx, by, c)
    y_peer = device(a, bx, ny, c)

    def group_peer(flips):
        fx, fy, fc = flips // 4, flips // 2 % 2, flips % 2
        x_at, y_at, c_at = (nx if fx else bx), (ny if fy else by), (nc if fc else c)
        return device(a, x_at, y_at, c_at), x_at * 4 + y_at * 2 + c_at

    def ring_peer(step):
        a_at = lax.rem(a + step, ring)
        return device(a_at, bx, by, c), a_at

    def each_ring(act):
        if ring <= 8:
            for step in range(1, ring):
                act(step)
        else:

            def go(step, _):
                act(step)
                return 0

            lax.fori_loop(1, ring, go, 0)

    def remote(src, dst, sems, at, target):
        return pltpu.make_async_remote_copy(
            src_ref=src,
            dst_ref=dst,
            send_sem=sems.at[(0,) + at],
            recv_sem=sems.at[(1,) + at],
            device_id=target,
            device_id_type=MESH,
        )

    barrier = pltpu.get_barrier_semaphore()
    for flips in range(1, 8):
        pl.semaphore_signal(barrier, 1, device_id=group_peer(flips)[0], device_id_type=MESH)
    each_ring(
        lambda step: pl.semaphore_signal(
            barrier, 1, device_id=ring_peer(step)[0], device_id_type=MESH
        )
    )

    def load_weight(layer, at):
        return pltpu.make_async_copy(weights.at[layer], wbuf, sem_w.at[at])

    load_weight(0, 0).start()

    x0f[:, pl.ds(hidden - hidden % LANES, width - hidden + hidden % LANES)] = jnp.zeros(
        (rows, width - hidden + hidden % LANES), F32
    )
    x0f[:, :hidden] = frames[...].astype(F32)
    params[...] = jnp.zeros(params.shape, F32)
    for at, source in enumerate((gain, shift, decay)):
        params[at * 2 : at * 2 + 2, :hidden] = source[...]
    pl.semaphore_wait(barrier, 7 + ring - 1)

    pair_peer = (x_peer, y_peer)
    other_peer = (y_peer, x_peer)
    pair_at = (bx, by)
    other_at = (by, bx)
    far_pair = (nx, ny)
    diagonal = (device(a, nx, by, nc), device(a, bx, ny, nc))
    sent_x = (x0f, x1r)

    def send_x(layer):
        to_pair = remote(sent_x[layer], xr.at[layer, 0], sem_x, (layer, 0), pair_peer[layer])
        to_core = remote(sent_x[layer], xr.at[layer, 1], sem_x, (layer, 1), core_peer)
        to_pair.start()
        to_core.start()

    def forward_x(layer):
        remote(sent_x[layer], xr.at[layer, 0], sem_x, (layer, 0), pair_peer[layer]).wait_recv()
        remote(xr.at[layer, 0], xr.at[layer, 2], sem_x, (layer, 2), core_peer).start()

    send_x(0)

    row_at = lax.broadcasted_iota(jnp.int32, (8, LANES), 0)
    length = lengths[0]

    def lanes_of(step):
        return pl.ds(pl.multiple_of(step * LANES, LANES), LANES)

    def over_lanes(act):
        def go(step, _):
            act(lanes_of(step), step)
            return 0

        lax.fori_loop(0, lane_steps, go, 0)

    def valid_at(block):
        return (row_at + block * 8) < length

    def spread(row):
        return jnp.broadcast_to(row, (8, LANES))

    def row_powers(decay_row, reverse):
        one = spread(decay_row)
        two = one * one
        four = two * two
        from_edge = 7 - row_at if reverse else row_at
        ones = jnp.ones((8, LANES), F32)
        power = (
            one
            * jnp.where(from_edge % 2 == 1, one, ones)
            * jnp.where(from_edge // 2 % 2 == 1, two, ones)
            * jnp.where(from_edge // 4 == 1, four, ones)
        )
        zero = jnp.zeros((8, LANES), F32)
        return (
            jnp.where(from_edge >= 1, one, zero),
            jnp.where(from_edge >= 2, two, zero),
            jnp.where(from_edge >= 4, four, zero),
            power,
        )

    def scan_blocks(values, powers, reverse):
        one, two, four, power = powers
        count = len(values)
        order = range(count - 1, -1, -1) if reverse else range(count)
        result = [None] * count
        carry = None
        for at in order:
            value = values[at]
            for amount, factor in ((1, one), (2, two), (4, four)):
                value = value + factor * pltpu.roll(value, 8 - amount if reverse else amount, 0)
            if carry is not None:
                value = value + power * carry
            carry = spread(value[0:1] if reverse else value[7:8])
            result[at] = value
        return result

    def project(layer, source):
        for at in range(0, hidden, quarter):
            span = min(quarter, hidden - at)
            normed[layer, :, at : at + span] = jnp.dot(
                source[:, :hidden], wbuf[:, at : at + span], preferred_element_type=F32
            )
        tail = hidden - hidden % LANES
        if tail < hidden:
            kept = normed[layer, :, tail:width]
            lane = lax.broadcasted_iota(jnp.int32, kept.shape, 1)
            normed[layer, :, tail:width] = jnp.where(lane < hidden - tail, kept, 0.0)

    mine = bx * 4 + by * 2 + c

    def moments(layer):
        frame_count = (views * length).astype(F32)

        def act(lanes, step):
            first = jnp.zeros((8, LANES), F32)
            square = jnp.zeros((8, LANES), F32)
            for view in range(views):
                for block in range(blocks):
                    value = normed[layer, view * slots + block * 8 : view * slots + block * 8 + 8, lanes]
                    value = jnp.where(valid_at(block), value, 0.0)
                    first += value
                    square += value * value
            first = jnp.sum(first, axis=0, keepdims=True)
            lane = lax.broadcasted_iota(jnp.int32, (1, LANES), 1) + step * LANES
            first = jnp.where(lane >= hidden, frame_count, first)
            eight_f[layer, mine, 0:1, lanes] = first
            eight_f[layer, mine, 1:2, lanes] = jnp.sum(square, axis=0, keepdims=True)

        over_lanes(act)

    def start_sum(eight, at):
        for flips in range(1, 8):
            peer, _ = group_peer(flips)
            remote(eight.at[mine], eight.at[mine], sem_e, (at, flips - 1), peer).start()

    def middle_sum(eight, around, at):
        for flips in range(1, 8):
            peer, slot = group_peer(flips)
            remote(eight.at[mine], eight.at[slot], sem_e, (at, flips - 1), peer).wait_recv()
        total = eight[0]
        for slot in range(1, 8):
            total = total + eight[slot]
        around[a] = total

        def send(step):
            peer, _ = ring_peer(step)
            remote(around.at[a], around.at[a], sem_r, (at, step), peer).start()

        each_ring(send)

    def finish_sum(eight, around, at, result):
        def wait(step):
            behind = lax.rem(a + ring - step, ring)
            remote(
                around.at[a], around.at[behind], sem_r, (at, step), device(behind, bx, by, c)
            ).wait_recv()

        each_ring(wait)
        total = around[0]
        for slot in range(1, ring):
            total = total + around[slot]
        result[...] = total

    def statistics(layer, lanes):
        count = jnp.broadcast_to(total_f[layer, 0:1, width - 1 : width], (1, LANES))
        average = total_f[layer, 0:1, lanes] / count
        variance = total_f[layer, 1:2, lanes] / count - average * average
        return average, lax.rsqrt(variance + EPS), count

    def forward(layer):
        def act(lanes, step):
            average, inverse, _ = statistics(layer, lanes)
            coef[layer : layer + 1, lanes] = inverse
            average, inverse = spread(average), spread(inverse)
            gain_row = spread(params[layer : layer + 1, lanes])
            shift_row = spread(params[2 + layer : 3 + layer, lanes])
            powers = row_powers(params[4 + layer : 5 + layer, lanes], False)
            for view in range(views):
                drives = []
                for block in range(blocks):
                    at = view * slots + block * 8
                    value = (normed[layer, at : at + 8, lanes] - average) * inverse
                    normed[layer, at : at + 8, lanes] = value
                    drives.append(gain_row * value + shift_row)
                result = scan_blocks(drives, powers, False)
                for block in range(blocks):
                    at = view * slots + block * 8
                    state = result[block]
                    states[layer, at : at + 8, lanes] = state
                    bump = jnp.maximum(state, 0.0) + jnp.log1p(jnp.exp(-jnp.abs(state)))
                    bump = jnp.where(valid_at(block), bump, 0.0)
                    if layer == 0:
                        following = x0f[at : at + 8, lanes] + bump
                        x1[at : at + 8, lanes] = following
                        x1r[at : at + 8, lanes] = following.astype(BF16).astype(F32)
                    else:
                        x1[at : at + 8, lanes] = x1[at : at + 8, lanes] + bump

        over_lanes(act)

    def backward_sums(layer):
        def act(lanes, step):
            powers = row_powers(params[4 + layer : 5 + layer, lanes], True)
            sums = [jnp.zeros((8, LANES), F32) for _ in range(3)]
            for view in range(views):
                sources = []
                kept = []
                for block in range(blocks):
                    at = view * slots + block * 8
                    state = states[layer, at : at + 8, lanes]
                    kept.append(state)
                    slope = 1.0 / (1.0 + jnp.exp(-state))
                    slope = gy[at : at + 8, lanes] * slope
                    sources.append(jnp.where(valid_at(block), slope, 0.0))
                carried = scan_blocks(sources, powers, True)
                for block in range(blocks):
                    at = view * slots + block * 8
                    value = carried[block]
                    gpf[layer, at : at + 8, lanes] = value
                    shifted = pltpu.roll(kept[block], 1, 0)
                    before = spread(kept[block - 1][7:8]) if block else jnp.zeros((8, LANES), F32)
                    shifted = jnp.where(row_at == 0, before, shifted)
                    sums[0] += value * normed[layer, at : at + 8, lanes]
                    sums[1] += value
                    sums[2] += value * shifted
            for at in range(3):
                eight_b[layer, mine, at : at + 1, lanes] = jnp.sum(sums[at], axis=0, keepdims=True)
            eight_b[layer, mine, 3:4, lanes] = jnp.zeros((1, LANES), F32)

        over_lanes(act)

    def backward_drive(layer):
        grad_gain[layer : layer + 1, :] = total_b[layer, 0:1, :hidden]
        grad_shift[layer : layer + 1, :] = total_b[layer, 1:2, :hidden]
        grad_decay[layer : layer + 1, :] = total_b[layer, 2:3, :hidden]

        def act(lanes, step):
            count = jnp.broadcast_to(total_f[layer, 0:1, width - 1 : width], (1, LANES))
            slope = spread(total_b[layer, 0:1, lanes] / count)
            offset = spread(total_b[layer, 1:2, lanes] / count)
            scale = spread(coef[layer : layer + 1, lanes] * params[layer : layer + 1, lanes])
            for view in range(views):
                for block in range(0, blocks, 2):
                    pair = []
                    for side in range(2):
                        at = view * slots + (block + side) * 8
                        drop = offset + normed[layer, at : at + 8, lanes] * slope
                        drop = jnp.where(valid_at(block + side), drop, 0.0)
                        pair.append(scale * (gpf[layer, at : at + 8, lanes] - drop))
                    at = view * slots + block * 8
                    low = jnp.concatenate(pair, axis=0).astype(BF16)
                    gpb[at : at + 16, lanes] = low
                    gpf[layer, at : at + 16, lanes] = low.astype(F32)

        over_lanes(act)

    def quarter_at(p_at, c_at):
        return pl.ds(pl.multiple_of((p_at * 2 + c_at) * quarter, quarter), quarter)

    def grad_copies(layer):
        own, far = pair_at[layer], far_pair[layer]
        return [
            remote(gpf.at[layer, :, quarter_at(p_at, c_at)], gr.at[layer, at], sem_g, (layer, at), peer)
            for at, (p_at, c_at, peer) in enumerate(
                ((far, c, pair_peer[layer]), (own, nc, core_peer), (far, nc, diagonal[layer]))
            )
        ]

    def back_project():
        for at in range(0, hidden, quarter):
            span = min(quarter, hidden - at)
            gy[:, at : at + span] += lax.dot_general(
                gpb[:, :hidden],
                wbuf[at : at + span, :],
                (((1,), (1,)), ((), ())),
                preferred_element_type=F32,
            )

    def wait_factors(layer):
        remote(sent_x[layer], xr.at[layer, 1], sem_x, (layer, 1), core_peer).wait_recv()
        remote(xr.at[layer, 0], xr.at[layer, 2], sem_x, (layer, 2), core_peer).wait_recv()
        for copy in grad_copies(layer):
            copy.wait_recv()

    def weight_product(layer):
        gb[0:rows, :] = gpf[layer, :, quarter_at(pair_at[layer], c)].astype(BF16)
        for at in range(3):
            gb[(at + 1) * rows : (at + 2) * rows, :] = gr[layer, at].astype(BF16)
        for start in range(0, width, quarter):
            span = min(quarter, padded - start)
            xchunk[0:rows, :] = sent_x[layer][:, start : start + quarter].astype(BF16)
            for at in range(3):
                xchunk[(at + 1) * rows : (at + 2) * rows, :] = xr[
                    layer, at, :, start : start + quarter
                ].astype(BF16)
            product = lax.dot_general(
                xchunk[...], gb[...], (((0,), (0,)), ((), ())), preferred_element_type=F32
            )
            dw[layer, start : start + span, :] = product[:span]
        if padded > width:
            dw[layer, width:padded, :] = jnp.zeros((padded - width, quarter), F32)

    def half_at(o_at):
        return pl.ds(pl.multiple_of(o_at * half, half), half)

    def dw_parts(layer):
        return dw.at[layer].reshape(ring, chunks, chunk_rows, quarter)

    def copy_half(layer, k):
        return remote(
            dw_parts(layer).at[:, k, :, half_at(1 - other_at[layer])],
            ro.at[layer, :, k],
            sem_ro,
            (layer, k),
            other_peer[layer],
        )

    def reduce_half(layer, k):
        copy_half(layer, k).wait_recv()
        for at in range(ring):
            start = (at * chunks + k) * chunk_rows
            ro[layer, at, k] = (
                ro[layer, at, k] + dw[layer, start : start + chunk_rows, half_at(other_at[layer])]
            )

        def send(step):
            peer, a_at = ring_peer(step)
            remote(
                ro.at[layer, a_at, k], ra.at[layer, a, k], sem_ra, (layer, k, step), peer
            ).start()

        each_ring(send)

    def column(layer, p_at, o_at, c_at):
        return pl.ds(pl.multiple_of((p_at * 2 + c_at) * quarter + o_at * half, half), half)

    def own_column(layer):
        return column(layer, pair_at[layer], other_at[layer], c)

    def reduce_ring(layer, k):
        def wait(step):
            behind = lax.rem(a + ring - step, ring)
            remote(
                ro.at[layer, a, k],
                ra.at[layer, behind, k],
                sem_ra,
                (layer, k, step),
                device(behind, bx, by, c),
            ).wait_recv()

        each_ring(wait)

        def add(step, total):
            return total + ra[layer, lax.rem(a + step, ring), k]

        total = ro[layer, a, k]
        if ring <= 8:
            for step in range(1, ring):
                total = add(step, total)
        else:
            total = lax.fori_loop(1, ring, add, total)
        ro[layer, a, k] = total
        local_copy(layer, k).start()

        def send(step):
            peer, _ = ring_peer(step)
            remote(
                ro.at[layer, a, k],
                grad_weights.at[layer, a, k, :, own_column(layer)],
                sem_aa,
                (layer, k, step),
                peer,
            ).start()

        each_ring(send)

    def local_copy(layer, k):
        return pltpu.make_async_copy(
            ro.at[layer, a, k],
            grad_weights.at[layer, a, k, :, own_column(layer)],
            sem_l.at[layer, k],
        )

    def gathered(layer, k, p_at, o_at, c_at):
        return grad_weights.at[layer, :, k, :, column(layer, p_at, o_at, c_at)]

    def order_of(layer, k):
        pair_first = (k + layer) % 2 == 1
        own = (pair_at[layer], other_at[layer])
        flip_p = (far_pair[layer], other_at[layer])
        flip_o = (pair_at[layer], 1 - other_at[layer])
        both = (far_pair[layer], 1 - other_at[layer])
        if pair_first:
            return (own, flip_p, flip_o, both), pair_peer[layer], other_peer[layer]
        return (own, flip_o, flip_p, both), other_peer[layer], pair_peer[layer]

    def block_copy(layer, k, kind):
        spots, first, second = order_of(layer, k)
        spot, peer = {
            0: (0, first),
            1: (0, second),
            2: (1, second),
            3: (0, core_peer),
            4: (1, core_peer),
            5: (2, core_peer),
            6: (3, core_peer),
        }[kind]
        region = gathered(layer, k, *spots[spot], c)
        return remote(region, region, sem_ag, (layer, k, kind), peer)

    def arrived(layer, k, kind):
        spots, first, second = order_of(layer, k)
        spot = {0: 1, 1: 2, 2: 3, 3: 0, 4: 1, 5: 2, 6: 3}[kind]
        region = gathered(layer, k, *spots[spot], nc if kind >= 3 else c)
        remote(region, region, sem_ag, (layer, k, kind), core_peer).wait_recv()

    def gather_ring(layer, k):
        def wait(step):
            behind = lax.rem(a + ring - step, ring)
            remote(
                ro.at[layer, a, k],
                grad_weights.at[layer, behind, k, :, own_column(layer)],
                sem_aa,
                (layer, k, step),
                device(behind, bx, by, c),
            ).wait_recv()

        each_ring(wait)
        local_copy(layer, k).wait()
        block_copy(layer, k, 0).start()
        block_copy(layer, k, 1).start()
        block_copy(layer, k, 3).start()

    def gather_first(layer, k):
        arrived(layer, k, 0)
        block_copy(layer, k, 2).start()
        block_copy(layer, k, 4).start()

    def gather_second(layer, k):
        arrived(layer, k, 1)
        block_copy(layer, k, 5).start()
        arrived(layer, k, 2)
        block_copy(layer, k, 6).start()

    xb[...] = x0f[...].astype(BF16)
    load_weight(0, 0).wait()
    project(0, xb)
    load_weight(1, 1).start()
    moments(0)
    start_sum(eight_f.at[0], 0)
    gy[:, pl.ds(hidden - hidden % LANES, width - hidden + hidden % LANES)] = jnp.zeros(
        (rows, width - hidden + hidden % LANES), F32
    )
    gy[:, :hidden] = cotangent[...].astype(F32)
    middle_sum(eight_f.at[0], ring_f.at[0], 0)
    finish_sum(eight_f.at[0], ring_f.at[0], 0, total_f.at[0])
    forward(0)
    send_x(1)
    xb[...] = x1r[...].astype(BF16)
    load_weight(1, 1).wait()
    project(1, xb)
    moments(1)
    start_sum(eight_f.at[1], 1)
    middle_sum(eight_f.at[1], ring_f.at[1], 1)
    finish_sum(eight_f.at[1], ring_f.at[1], 1, total_f.at[1])
    forward(1)
    backward_sums(1)
    start_sum(eight_b.at[1], 2)
    output[...] = x1[:, :hidden].astype(BF16)
    middle_sum(eight_b.at[1], ring_b.at[1], 2)
    finish_sum(eight_b.at[1], ring_b.at[1], 2, total_b.at[1])
    backward_drive(1)
    for copy in grad_copies(1):
        copy.start()
    back_project()
    load_weight(0, 2).start()
    backward_sums(0)
    start_sum(eight_b.at[0], 3)
    forward_x(0)
    middle_sum(eight_b.at[0], ring_b.at[0], 3)
    finish_sum(eight_b.at[0], ring_b.at[0], 3, total_b.at[0])
    backward_drive(0)
    for copy in grad_copies(0):
        copy.start()
    forward_x(1)
    wait_factors(1)
    weight_product(1)
    for k in range(chunks):
        copy_half(1, k).start()
    load_weight(0, 2).wait()
    back_project()
    grad_frames[...] = gy[:, :hidden].astype(BF16)
    wait_factors(0)
    weight_product(0)
    for k in range(chunks):
        copy_half(0, k).start()

    stages = (reduce_half, reduce_ring, gather_ring, gather_first, gather_second)
    tasks = []
    for layer in (1, 0):
        for k in range(chunks):
            for at, stage in enumerate(stages):
                tasks.append(((1 - layer) * chunks + k + at, at, layer, k, stage))
    tasks.sort(key=lambda task: (task[0], -task[1]))
    for _, _, layer, k, stage in tasks:
        stage(layer, k)

    for layer in (1, 0):
        for k in range(chunks):
            for kind in range(3, 7):
                arrived(layer, k, kind)
    for layer in range(2):
        remote(sent_x[layer], xr.at[layer, 0], sem_x, (layer, 0), pair_peer[layer]).wait_send()
        remote(sent_x[layer], xr.at[layer, 1], sem_x, (layer, 1), core_peer).wait_send()
        remote(xr.at[layer, 0], xr.at[layer, 2], sem_x, (layer, 2), core_peer).wait_send()
        for copy in grad_copies(layer):
            copy.wait_send()
        for k in range(chunks):
            copy_half(layer, k).wait_send()

            def wait(step):
                peer, a_at = ring_peer(step)
                remote(
                    ro.at[layer, a_at, k], ra.at[layer, a, k], sem_ra, (layer, k, step), peer
                ).wait_send()
                remote(
                    ro.at[layer, a, k],
                    grad_weights.at[layer, a, k, :, own_column(layer)],
                    sem_aa,
                    (layer, k, step),
                    peer,
                ).wait_send()

            each_ring(wait)
            for kind in range(7):
                block_copy(layer, k, kind).wait_send()
    for at, eight, around in (
        (0, eight_f.at[0], ring_f.at[0]),
        (1, eight_f.at[1], ring_f.at[1]),
        (2, eight_b.at[1], ring_b.at[1]),
        (3, eight_b.at[0], ring_b.at[0]),
    ):
        for flips in range(1, 8):
            peer, _ = group_peer(flips)
            remote(eight.at[mine], eight.at[mine], sem_e, (at, flips - 1), peer).wait_send()

        def wait_sum(step):
            peer, _ = ring_peer(step)
            remote(around.at[a], around.at[a], sem_r, (at, step), peer).wait_send()

        each_ring(wait_sum)


def body(ring, frames, weights, norm_gain, norm_shift, decays, lengths, cotangent):
    _, views, slots, hidden = frames.shape
    width = round_up(hidden, 4 * LANES)
    rows = views * slots
    padded, chunks, chunk_rows = pick_chunks(hidden, ring)
    dims = (ring, chunks, chunk_rows, views, slots, hidden, width)
    quarter = width // 4
    half = quarter // 2
    vmem = pl.BlockSpec(memory_space=pltpu.VMEM)
    anywhere = pl.BlockSpec(memory_space=pl.ANY)
    scratch = [
        pltpu.VMEM((hidden, hidden), BF16),
        pltpu.VMEM((rows, width), F32),
        pltpu.VMEM((rows, width), F32),
        pltpu.VMEM((rows, width), F32),
        pltpu.VMEM((rows, width), BF16),
        pltpu.VMEM((2, rows, width), F32),
        pltpu.VMEM((2, rows, width), F32),
        pltpu.VMEM((rows, width), F32),
        pltpu.VMEM((2, rows, width), F32),
        pltpu.VMEM((rows, width), BF16),
        pltpu.VMEM((2, 3, rows, width), F32),
        pltpu.VMEM((2, 3, rows, quarter), F32),
        pltpu.VMEM((4 * rows, quarter), BF16),
        pltpu.VMEM((4 * rows, quarter), BF16),
        pltpu.VMEM((2, padded, quarter), F32),
        pltpu.VMEM((2, ring, chunks, chunk_rows, half), F32),
        pltpu.VMEM((2, ring, chunks, chunk_rows, half), F32),
        pltpu.VMEM((8, width), F32),
        pltpu.VMEM((2, width), F32),
        pltpu.VMEM((2, 8, 2, width), F32),
        pltpu.VMEM((2, 8, 4, width), F32),
        pltpu.VMEM((2, ring, 2, width), F32),
        pltpu.VMEM((2, ring, 4, width), F32),
        pltpu.VMEM((2, 2, width), F32),
        pltpu.VMEM((2, 4, width), F32),
        pltpu.SemaphoreType.DMA((3,)),
        pltpu.SemaphoreType.DMA((2, 2, 3)),
        pltpu.SemaphoreType.DMA((2, 2, 3)),
        pltpu.SemaphoreType.DMA((2, 4, 7)),
        pltpu.SemaphoreType.DMA((2, 4, ring)),
        pltpu.SemaphoreType.DMA((2, 2, chunks)),
        pltpu.SemaphoreType.DMA((2, 2, chunks, ring)),
        pltpu.SemaphoreType.DMA((2, 2, chunks, ring)),
        pltpu.SemaphoreType.DMA((2, 2, chunks, 7)),
        pltpu.SemaphoreType.DMA((2, chunks)),
    ]
    small = jax.ShapeDtypeStruct((2, hidden), F32)
    flat = jax.ShapeDtypeStruct((rows, hidden), BF16)
    result, grad_first, grad_weights, grad_gain, grad_shift, grad_decay = pl.pallas_call(
        functools.partial(kernel, dims),
        out_shape=(
            flat,
            flat,
            jax.ShapeDtypeStruct((2, ring, chunks, chunk_rows, width), F32),
            small,
            small,
            small,
        ),
        in_specs=[
            vmem,
            anywhere,
            vmem,
            vmem,
            vmem,
            pl.BlockSpec(memory_space=pltpu.SMEM),
            vmem,
        ],
        out_specs=(vmem, vmem, anywhere, vmem, vmem, vmem),
        scratch_shapes=scratch,
        compiler_params=pltpu.CompilerParams(
            collective_id=0, has_side_effects=True, vmem_limit_bytes=60 << 20
        ),
    )(
        frames.reshape(rows, hidden),
        weights,
        norm_gain,
        norm_shift,
        decays,
        lengths,
        cotangent.reshape(rows, hidden),
    )
    grad_weights = grad_weights.reshape(2, padded, width)[:, :hidden, :hidden]
    return (
        result.reshape(frames.shape),
        grad_first.reshape(frames.shape),
        grad_weights,
        grad_gain,
        grad_shift,
        grad_decay,
    )


def solution(mesh):
    everywhere = P(("dp", "rep"), None, None, None)
    return jax.shard_map(
        functools.partial(body, mesh.shape["dp"] // 2),
        mesh=mesh,
        in_specs=(everywhere, P(), P(), P(), P(), P(("dp", "rep")), everywhere),
        out_specs=(everywhere, everywhere, P(), P(), P(), P()),
        check_vma=False,
    )
```

```python
import functools

import jax
import jax.numpy as jnp
from jax import lax
from jax.experimental import pallas as pl
from jax.experimental.pallas import tpu as pltpu
from jax.sharding import PartitionSpec as P

EPS = 1e-05
MESH = pl.DeviceIdType.MESH
F32 = jnp.float32
BF16 = jnp.bfloat16
DELAY = 8
LANES = 128


def round_up(value, unit):
    return -(-value // unit) * unit


def chunk_plan(hidden, ring, step):
    plan, start = [], 0
    while start < hidden:
        span = min(step, round_up(hidden - start, 8 * ring))
        plan.append((start, span // ring))
        start += span
    return tuple(plan), start


def kernel(
    dims,
    frames,
    weights,
    gain,
    shift,
    decay,
    lengths,
    cotangent,
    output,
    grad_frames,
    grad_weights,
    grad_gain,
    grad_shift,
    grad_decay,
    wbuf,
    x0f,
    x1,
    x1r,
    xb,
    normed,
    states,
    gy,
    gpf,
    gpb,
    xr,
    gr,
    xchunk,
    gb,
    dw,
    ro,
    ra,
    params,
    coef,
    eight_f,
    eight_b,
    ring_f,
    ring_b,
    total_f,
    total_b,
    sem_w,
    sem_x,
    sem_g,
    sem_e,
    sem_r,
    sem_ro,
    sem_ra,
    sem_aa,
    sem_ag,
    sem_l,
):
    ring, plan, padded, step_rows, views, slots, hidden, width = dims
    chunks = len(plan)
    rows = views * slots
    quarter = width // 4
    half = quarter // 2
    blocks = slots // 8
    lane_steps = width // LANES

    dp, rep = lax.axis_index("dp"), lax.axis_index("rep")
    a, bx = dp // 2, dp % 2
    by, c = rep // 2, rep % 2
    nx, ny, nc = 1 - bx, 1 - by, 1 - c

    def device(a_at, x_at, y_at, c_at):
        return (a_at * 2 + x_at, y_at * 2 + c_at)

    core_peer = device(a, bx, by, nc)
    x_peer = device(a, nx, by, c)
    y_peer = device(a, bx, ny, c)

    def group_peer(flips):
        fx, fy, fc = flips // 4, flips // 2 % 2, flips % 2
        x_at, y_at, c_at = (nx if fx else bx), (ny if fy else by), (nc if fc else c)
        return device(a, x_at, y_at, c_at), x_at * 4 + y_at * 2 + c_at

    def ring_peer(step):
        a_at = lax.rem(a + step, ring)
        return device(a_at, bx, by, c), a_at

    def each_ring(act):
        if ring <= 8:
            for step in range(1, ring):
                act(step)
        else:

            def go(step, _):
                act(step)
                return 0

            lax.fori_loop(1, ring, go, 0)

    def remote(src, dst, sems, at, target):
        return pltpu.make_async_remote_copy(
            src_ref=src,
            dst_ref=dst,
            send_sem=sems.at[(0,) + at],
            recv_sem=sems.at[(1,) + at],
            device_id=target,
            device_id_type=MESH,
        )

    barrier = pltpu.get_barrier_semaphore()
    for flips in range(1, 8):
        pl.semaphore_signal(barrier, 1, device_id=group_peer(flips)[0], device_id_type=MESH)
    each_ring(
        lambda step: pl.semaphore_signal(
            barrier, 1, device_id=ring_peer(step)[0], device_id_type=MESH
        )
    )

    def load_weight(layer, at):
        return pltpu.make_async_copy(weights.at[layer], wbuf, sem_w.at[at])

    load_weight(0, 0).start()

    x0f[:, pl.ds(hidden - hidden % LANES, width - hidden + hidden % LANES)] = jnp.zeros(
        (rows, width - hidden + hidden % LANES), F32
    )
    x0f[:, :hidden] = frames[...].astype(F32)
    params[...] = jnp.zeros(params.shape, F32)
    for at, source in enumerate((gain, shift, decay)):
        params[at * 2 : at * 2 + 2, :hidden] = source[...]
    pl.semaphore_wait(barrier, 7 + ring - 1)

    pair_peer = (x_peer, y_peer)
    other_peer = (y_peer, x_peer)
    pair_at = (bx, by)
    other_at = (by, bx)
    far_pair = (nx, ny)
    diagonal = (device(a, nx, by, nc), device(a, bx, ny, nc))
    sent_x = (x0f, x1r)

    def piece(k):
        return slice(k * step_rows, (k + 1) * step_rows)

    def x_copy(layer, k, kind):
        source = sent_x[layer].at[:, piece(k)] if kind < 2 else xr.at[layer, 0, :, piece(k)]
        return remote(
            source,
            xr.at[layer, kind, :, piece(k)],
            sem_x,
            (layer, k, kind),
            core_peer if kind else pair_peer[layer],
        )

    def send_x(layer, first, last):
        for k in range(first, last):
            x_copy(layer, k, 0).start()
            x_copy(layer, k, 1).start()

    def forward_x(layer, k):
        x_copy(layer, k, 0).wait_recv()
        x_copy(layer, k, 2).start()

    row_at = lax.broadcasted_iota(jnp.int32, (8, LANES), 0)
    length = lengths[0]

    def lanes_of(step):
        return pl.ds(pl.multiple_of(step * LANES, LANES), LANES)

    def over_lanes(act):
        def go(step, _):
            act(lanes_of(step), step)
            return 0

        lax.fori_loop(0, lane_steps, go, 0)

    def valid_at(block):
        return (row_at + block * 8) < length

    def spread(row):
        return jnp.broadcast_to(row, (8, LANES))

    def row_powers(decay_row, reverse):
        one = spread(decay_row)
        two = one * one
        four = two * two
        from_edge = 7 - row_at if reverse else row_at
        ones = jnp.ones((8, LANES), F32)
        power = (
            one
            * jnp.where(from_edge % 2 == 1, one, ones)
            * jnp.where(from_edge // 2 % 2 == 1, two, ones)
            * jnp.where(from_edge // 4 == 1, four, ones)
        )
        zero = jnp.zeros((8, LANES), F32)
        return (
            jnp.where(from_edge >= 1, one, zero),
            jnp.where(from_edge >= 2, two, zero),
            jnp.where(from_edge >= 4, four, zero),
            power,
        )

    def scan_blocks(values, powers, reverse):
        one, two, four, power = powers
        count = len(values)
        order = range(count - 1, -1, -1) if reverse else range(count)
        result = [None] * count
        carry = None
        for at in order:
            value = values[at]
            for amount, factor in ((1, one), (2, two), (4, four)):
                value = value + factor * pltpu.roll(value, 8 - amount if reverse else amount, 0)
            if carry is not None:
                value = value + power * carry
            carry = spread(value[0:1] if reverse else value[7:8])
            result[at] = value
        return result

    def project(layer, source):
        for at in range(0, hidden, quarter):
            span = min(quarter, hidden - at)
            normed[layer, :, at : at + span] = jnp.dot(
                source[:, :hidden], wbuf[:, at : at + span], preferred_element_type=F32
            )
        tail = hidden - hidden % LANES
        if tail < hidden:
            kept = normed[layer, :, tail:width]
            lane = lax.broadcasted_iota(jnp.int32, kept.shape, 1)
            normed[layer, :, tail:width] = jnp.where(lane < hidden - tail, kept, 0.0)

    mine = bx * 4 + by * 2 + c

    def moments(layer):
        frame_count = (views * length).astype(F32)

        def act(lanes, step):
            first = jnp.zeros((8, LANES), F32)
            square = jnp.zeros((8, LANES), F32)
            for view in range(views):
                for block in range(blocks):
                    value = normed[layer, view * slots + block * 8 : view * slots + block * 8 + 8, lanes]
                    value = jnp.where(valid_at(block), value, 0.0)
                    first += value
                    square += value * value
            first = jnp.sum(first, axis=0, keepdims=True)
            lane = lax.broadcasted_iota(jnp.int32, (1, LANES), 1) + step * LANES
            first = jnp.where(lane >= hidden, frame_count, first)
            eight_f[layer, mine, 0:1, lanes] = first
            eight_f[layer, mine, 1:2, lanes] = jnp.sum(square, axis=0, keepdims=True)

        over_lanes(act)

    def start_sum(eight, at):
        for flips in range(1, 8):
            peer, _ = group_peer(flips)
            remote(eight.at[mine], eight.at[mine], sem_e, (at, flips - 1), peer).start()

    def middle_sum(eight, around, at):
        for flips in range(1, 8):
            peer, slot = group_peer(flips)
            remote(eight.at[mine], eight.at[slot], sem_e, (at, flips - 1), peer).wait_recv()
        total = eight[0]
        for slot in range(1, 8):
            total = total + eight[slot]
        around[a] = total

        def send(step):
            peer, _ = ring_peer(step)
            remote(around.at[a], around.at[a], sem_r, (at, step), peer).start()

        each_ring(send)

    def finish_sum(eight, around, at, result):
        def wait(step):
            behind = lax.rem(a + ring - step, ring)
            remote(
                around.at[a], around.at[behind], sem_r, (at, step), device(behind, bx, by, c)
            ).wait_recv()

        each_ring(wait)
        total = around[0]
        for slot in range(1, ring):
            total = total + around[slot]
        result[...] = total

    def statistics(layer, lanes):
        count = jnp.broadcast_to(total_f[layer, 0:1, width - 1 : width], (1, LANES))
        average = total_f[layer, 0:1, lanes] / count
        variance = total_f[layer, 1:2, lanes] / count - average * average
        return average, lax.rsqrt(variance + EPS), count

    def forward(layer):
        def act(lanes, step):
            average, inverse, _ = statistics(layer, lanes)
            coef[layer : layer + 1, lanes] = inverse
            average, inverse = spread(average), spread(inverse)
            gain_row = spread(params[layer : layer + 1, lanes])
            shift_row = spread(params[2 + layer : 3 + layer, lanes])
            powers = row_powers(params[4 + layer : 5 + layer, lanes], False)
            for view in range(views):
                drives = []
                for block in range(blocks):
                    at = view * slots + block * 8
                    value = (normed[layer, at : at + 8, lanes] - average) * inverse
                    normed[layer, at : at + 8, lanes] = value
                    drives.append(gain_row * value + shift_row)
                result = scan_blocks(drives, powers, False)
                for block in range(blocks):
                    at = view * slots + block * 8
                    state = result[block]
                    states[layer, at : at + 8, lanes] = state
                    bump = jnp.maximum(state, 0.0) + jnp.log1p(jnp.exp(-jnp.abs(state)))
                    bump = jnp.where(valid_at(block), bump, 0.0)
                    if layer == 0:
                        following = x0f[at : at + 8, lanes] + bump
                        x1[at : at + 8, lanes] = following
                        x1r[at : at + 8, lanes] = following.astype(BF16).astype(F32)
                    else:
                        x1[at : at + 8, lanes] = x1[at : at + 8, lanes] + bump

        over_lanes(act)

    def backward_sums(layer):
        def act(lanes, step):
            powers = row_powers(params[4 + layer : 5 + layer, lanes], True)
            sums = [jnp.zeros((8, LANES), F32) for _ in range(3)]
            for view in range(views):
                sources = []
                kept = []
                for block in range(blocks):
                    at = view * slots + block * 8
                    state = states[layer, at : at + 8, lanes]
                    kept.append(state)
                    slope = 1.0 / (1.0 + jnp.exp(-state))
                    slope = gy[at : at + 8, lanes] * slope
                    sources.append(jnp.where(valid_at(block), slope, 0.0))
                carried = scan_blocks(sources, powers, True)
                for block in range(blocks):
                    at = view * slots + block * 8
                    value = carried[block]
                    gpf[layer, at : at + 8, lanes] = value
                    shifted = pltpu.roll(kept[block], 1, 0)
                    before = spread(kept[block - 1][7:8]) if block else jnp.zeros((8, LANES), F32)
                    shifted = jnp.where(row_at == 0, before, shifted)
                    sums[0] += value * normed[layer, at : at + 8, lanes]
                    sums[1] += value
                    sums[2] += value * shifted
            for at in range(3):
                eight_b[layer, mine, at : at + 1, lanes] = jnp.sum(sums[at], axis=0, keepdims=True)
            eight_b[layer, mine, 3:4, lanes] = jnp.zeros((1, LANES), F32)

        over_lanes(act)

    def backward_drive(layer):
        grad_gain[layer : layer + 1, :] = total_b[layer, 0:1, :hidden]
        grad_shift[layer : layer + 1, :] = total_b[layer, 1:2, :hidden]
        grad_decay[layer : layer + 1, :] = total_b[layer, 2:3, :hidden]

        def act(lanes, step):
            count = jnp.broadcast_to(total_f[layer, 0:1, width - 1 : width], (1, LANES))
            slope = spread(total_b[layer, 0:1, lanes] / count)
            offset = spread(total_b[layer, 1:2, lanes] / count)
            scale = spread(coef[layer : layer + 1, lanes] * params[layer : layer + 1, lanes])
            for view in range(views):
                for block in range(0, blocks, 2):
                    pair = []
                    for side in range(2):
                        at = view * slots + (block + side) * 8
                        drop = offset + normed[layer, at : at + 8, lanes] * slope
                        drop = jnp.where(valid_at(block + side), drop, 0.0)
                        pair.append(scale * (gpf[layer, at : at + 8, lanes] - drop))
                    at = view * slots + block * 8
                    low = jnp.concatenate(pair, axis=0).astype(BF16)
                    gpb[at : at + 16, lanes] = low
                    gpf[layer, at : at + 16, lanes] = low.astype(F32)

        over_lanes(act)

    def quarter_at(p_at, c_at):
        return pl.ds(pl.multiple_of((p_at * 2 + c_at) * quarter, quarter), quarter)

    def grad_copies(layer):
        own, far = pair_at[layer], far_pair[layer]
        return [
            remote(gpf.at[layer, :, quarter_at(p_at, c_at)], gr.at[layer, at], sem_g, (layer, at), peer)
            for at, (p_at, c_at, peer) in enumerate(
                ((far, c, pair_peer[layer]), (own, nc, core_peer), (far, nc, diagonal[layer]))
            )
        ]

    def back_project():
        for at in range(0, hidden, quarter):
            span = min(quarter, hidden - at)
            gy[:, at : at + span] += lax.dot_general(
                gpb[:, :hidden],
                wbuf[at : at + span, :],
                (((1,), (1,)), ((), ())),
                preferred_element_type=F32,
            )

    def load_factors(layer):
        for copy in grad_copies(layer):
            copy.wait_recv()
        gb[0:rows, :] = gpf[layer, :, quarter_at(pair_at[layer], c)].astype(BF16)
        for at in range(3):
            gb[(at + 1) * rows : (at + 2) * rows, :] = gr[layer, at].astype(BF16)

    def weight_product(layer, k):
        x_copy(layer, k, 1).wait_recv()
        x_copy(layer, k, 2).wait_recv()
        start, shard = plan[k]
        span = ring * shard
        xchunk[0:rows, :] = sent_x[layer][:, piece(k)].astype(BF16)
        for at in range(3):
            xchunk[(at + 1) * rows : (at + 2) * rows, :] = xr[layer, at, :, piece(k)].astype(BF16)
        product = lax.dot_general(
            xchunk[...], gb[...], (((0,), (0,)), ((), ())), preferred_element_type=F32
        )
        dw[layer, start : start + span, :] = product[:span]

    def weight_products(layer, first, last):
        if first == 0:
            load_factors(layer)
            forward_x(layer, 0)
        for k in range(first, last):
            if k + 1 < chunks:
                forward_x(layer, k + 1)
            weight_product(layer, k)
            copy_half(layer, k).start()

    def half_at(o_at):
        return pl.ds(pl.multiple_of(o_at * half, half), half)

    def all_rows(k):
        start, shard = plan[k]
        return slice(start, start + ring * shard)

    def shard_rows(k, a_at):
        start, shard = plan[k]
        return pl.ds(pl.multiple_of(start + a_at * shard, 8), shard)

    def copy_half(layer, k):
        return remote(
            dw.at[layer, all_rows(k), half_at(1 - other_at[layer])],
            ro.at[layer, all_rows(k)],
            sem_ro,
            (layer, k),
            other_peer[layer],
        )

    def reduce_half(layer, k):
        copy_half(layer, k).wait_recv()
        ro[layer, all_rows(k)] = (
            ro[layer, all_rows(k)] + dw[layer, all_rows(k), half_at(other_at[layer])]
        )

        def send(step):
            peer, a_at = ring_peer(step)
            remote(
                ro.at[layer, shard_rows(k, a_at)], ra.at[layer, shard_rows(k, a)], sem_ra, (layer, k, step), peer
            ).start()

        each_ring(send)

    def column(layer, p_at, o_at, c_at):
        return pl.ds(pl.multiple_of((p_at * 2 + c_at) * quarter + o_at * half, half), half)

    def own_column(layer):
        return column(layer, pair_at[layer], other_at[layer], c)

    def reduce_ring(layer, k):
        def wait(step):
            behind = lax.rem(a + ring - step, ring)
            remote(
                ro.at[layer, shard_rows(k, a)],
                ra.at[layer, shard_rows(k, behind)],
                sem_ra,
                (layer, k, step),
                device(behind, bx, by, c),
            ).wait_recv()

        each_ring(wait)

        def add(step, total):
            return total + ra[layer, shard_rows(k, lax.rem(a + step, ring))]

        total = ro[layer, shard_rows(k, a)]
        if ring <= 8:
            for step in range(1, ring):
                total = add(step, total)
        else:
            total = lax.fori_loop(1, ring, add, total)
        ro[layer, shard_rows(k, a)] = total
        local_copy(layer, k).start()

        def send(step):
            peer, _ = ring_peer(step)
            remote(
                ro.at[layer, shard_rows(k, a)],
                grad_weights.at[layer, shard_rows(k, a), own_column(layer)],
                sem_aa,
                (layer, k, step),
                peer,
            ).start()

        each_ring(send)

    def local_copy(layer, k):
        return pltpu.make_async_copy(
            ro.at[layer, shard_rows(k, a)],
            grad_weights.at[layer, shard_rows(k, a), own_column(layer)],
            sem_l.at[layer, k],
        )

    def gathered(layer, k, p_at, o_at, c_at):
        return grad_weights.at[layer, all_rows(k), column(layer, p_at, o_at, c_at)]

    def order_of(layer, k):
        pair_first = (k + layer) % 2 == 1
        own = (pair_at[layer], other_at[layer])
        flip_p = (far_pair[layer], other_at[layer])
        flip_o = (pair_at[layer], 1 - other_at[layer])
        both = (far_pair[layer], 1 - other_at[layer])
        if pair_first:
            return (own, flip_p, flip_o, both), pair_peer[layer], other_peer[layer]
        return (own, flip_o, flip_p, both), other_peer[layer], pair_peer[layer]

    def block_copy(layer, k, kind):
        spots, first, second = order_of(layer, k)
        spot, peer = {
            0: (0, first),
            1: (0, second),
            2: (1, second),
            3: (0, core_peer),
            4: (1, core_peer),
            5: (2, core_peer),
            6: (3, core_peer),
        }[kind]
        region = gathered(layer, k, *spots[spot], c)
        return remote(region, region, sem_ag, (layer, k, kind), peer)

    def arrived(layer, k, kind):
        spots, first, second = order_of(layer, k)
        spot = {0: 1, 1: 2, 2: 3, 3: 0, 4: 1, 5: 2, 6: 3}[kind]
        region = gathered(layer, k, *spots[spot], nc if kind >= 3 else c)
        remote(region, region, sem_ag, (layer, k, kind), core_peer).wait_recv()

    def gather_ring(layer, k):
        def wait(step):
            behind = lax.rem(a + ring - step, ring)
            remote(
                ro.at[layer, shard_rows(k, a)],
                grad_weights.at[layer, shard_rows(k, behind), own_column(layer)],
                sem_aa,
                (layer, k, step),
                device(behind, bx, by, c),
            ).wait_recv()

        each_ring(wait)
        local_copy(layer, k).wait()
        block_copy(layer, k, 0).start()
        block_copy(layer, k, 1).start()
        block_copy(layer, k, 3).start()

    def gather_first(layer, k):
        arrived(layer, k, 0)
        block_copy(layer, k, 2).start()
        block_copy(layer, k, 4).start()

    def gather_second(layer, k):
        arrived(layer, k, 1)
        block_copy(layer, k, 5).start()
        arrived(layer, k, 2)
        block_copy(layer, k, 6).start()

    def shares(at, count):
        return chunks * at // 8, chunks * count // 8

    send_x(0, *shares(0, 1))
    xb[...] = x0f[...].astype(BF16)
    load_weight(0, 0).wait()
    project(0, xb)
    load_weight(1, 1).start()
    moments(0)
    start_sum(eight_f.at[0], 0)
    send_x(0, *shares(1, 4))
    gy[:, pl.ds(hidden - hidden % LANES, width - hidden + hidden % LANES)] = jnp.zeros(
        (rows, width - hidden + hidden % LANES), F32
    )
    gy[:, :hidden] = cotangent[...].astype(F32)
    middle_sum(eight_f.at[0], ring_f.at[0], 0)
    finish_sum(eight_f.at[0], ring_f.at[0], 0, total_f.at[0])
    forward(0)
    send_x(1, *shares(0, 1))
    xb[...] = x1r[...].astype(BF16)
    load_weight(1, 1).wait()
    project(1, xb)
    moments(1)
    start_sum(eight_f.at[1], 1)
    send_x(1, *shares(1, 4))
    send_x(0, *shares(4, 6))
    middle_sum(eight_f.at[1], ring_f.at[1], 1)
    finish_sum(eight_f.at[1], ring_f.at[1], 1, total_f.at[1])
    forward(1)
    backward_sums(1)
    start_sum(eight_b.at[1], 2)
    send_x(1, *shares(4, 6))
    send_x(0, *shares(6, 8))
    output[...] = x1[:, :hidden].astype(BF16)
    middle_sum(eight_b.at[1], ring_b.at[1], 2)
    finish_sum(eight_b.at[1], ring_b.at[1], 2, total_b.at[1])
    backward_drive(1)
    for copy in grad_copies(1):
        copy.start()
    back_project()
    load_weight(0, 2).start()
    backward_sums(0)
    start_sum(eight_b.at[0], 3)
    send_x(1, *shares(6, 8))
    weight_products(1, *shares(0, 3))
    middle_sum(eight_b.at[0], ring_b.at[0], 3)
    finish_sum(eight_b.at[0], ring_b.at[0], 3, total_b.at[0])
    backward_drive(0)
    for copy in grad_copies(0):
        copy.start()
    weight_products(1, *shares(3, 8))
    load_weight(0, 2).wait()
    back_project()
    grad_frames[...] = gy[:, :hidden].astype(BF16)

    stages = (reduce_half, reduce_ring, gather_ring, gather_first, gather_second)
    lag = (0, 2, 4, 6, 9)
    tasks = []
    for layer in (1, 0):
        for k in range(chunks):
            for at, stage in enumerate(stages):
                due = 2 * k + lag[at] + (0 if layer else DELAY)
                tasks.append((due, -at, layer, k, stage))
    tasks.append((DELAY - 2, -9, 0, 0, lambda layer, k: weight_products(0, 0, chunks)))
    tasks.sort(key=lambda task: task[:2])
    for _, _, layer, k, stage in tasks:
        stage(layer, k)

    for layer in (1, 0):
        for k in range(chunks):
            for kind in range(3, 7):
                arrived(layer, k, kind)
    for layer in range(2):
        for k in range(chunks):
            for kind in range(3):
                x_copy(layer, k, kind).wait_send()
        for copy in grad_copies(layer):
            copy.wait_send()
        for k in range(chunks):
            copy_half(layer, k).wait_send()

            def wait(step):
                peer, a_at = ring_peer(step)
                remote(
                    ro.at[layer, shard_rows(k, a_at)], ra.at[layer, shard_rows(k, a)], sem_ra, (layer, k, step), peer
                ).wait_send()
                remote(
                    ro.at[layer, shard_rows(k, a)],
                    grad_weights.at[layer, shard_rows(k, a), own_column(layer)],
                    sem_aa,
                    (layer, k, step),
                    peer,
                ).wait_send()

            each_ring(wait)
            for kind in range(7):
                block_copy(layer, k, kind).wait_send()
    for at, eight, around in (
        (0, eight_f.at[0], ring_f.at[0]),
        (1, eight_f.at[1], ring_f.at[1]),
        (2, eight_b.at[1], ring_b.at[1]),
        (3, eight_b.at[0], ring_b.at[0]),
    ):
        for flips in range(1, 8):
            peer, _ = group_peer(flips)
            remote(eight.at[mine], eight.at[mine], sem_e, (at, flips - 1), peer).wait_send()

        def wait_sum(step):
            peer, _ = ring_peer(step)
            remote(around.at[a], around.at[a], sem_r, (at, step), peer).wait_send()

        each_ring(wait_sum)


def body(ring, frames, weights, norm_gain, norm_shift, decays, lengths, cotangent):
    _, views, slots, hidden = frames.shape
    width = round_up(hidden, 4 * LANES)
    rows = views * slots
    quarter = width // 4
    step_rows = width // 8
    plan, padded = chunk_plan(hidden, ring, step_rows)
    chunks = len(plan)
    dims = (ring, plan, padded, step_rows, views, slots, hidden, width)
    half = quarter // 2
    vmem = pl.BlockSpec(memory_space=pltpu.VMEM)
    anywhere = pl.BlockSpec(memory_space=pl.ANY)
    scratch = [
        pltpu.VMEM((hidden, hidden), BF16),
        pltpu.VMEM((rows, width), F32),
        pltpu.VMEM((rows, width), F32),
        pltpu.VMEM((rows, width), F32),
        pltpu.VMEM((rows, width), BF16),
        pltpu.VMEM((2, rows, width), F32),
        pltpu.VMEM((2, rows, width), F32),
        pltpu.VMEM((rows, width), F32),
        pltpu.VMEM((2, rows, width), F32),
        pltpu.VMEM((rows, width), BF16),
        pltpu.VMEM((2, 3, rows, width), F32),
        pltpu.VMEM((2, 3, rows, quarter), F32),
        pltpu.VMEM((4 * rows, step_rows), BF16),
        pltpu.VMEM((4 * rows, quarter), BF16),
        pltpu.VMEM((2, padded, quarter), F32),
        pltpu.VMEM((2, padded, half), F32),
        pltpu.VMEM((2, padded, half), F32),
        pltpu.VMEM((8, width), F32),
        pltpu.VMEM((2, width), F32),
        pltpu.VMEM((2, 8, 2, width), F32),
        pltpu.VMEM((2, 8, 4, width), F32),
        pltpu.VMEM((2, ring, 2, width), F32),
        pltpu.VMEM((2, ring, 4, width), F32),
        pltpu.VMEM((2, 2, width), F32),
        pltpu.VMEM((2, 4, width), F32),
        pltpu.SemaphoreType.DMA((3,)),
        pltpu.SemaphoreType.DMA((2, 2, chunks, 3)),
        pltpu.SemaphoreType.DMA((2, 2, 3)),
        pltpu.SemaphoreType.DMA((2, 4, 7)),
        pltpu.SemaphoreType.DMA((2, 4, ring)),
        pltpu.SemaphoreType.DMA((2, 2, chunks)),
        pltpu.SemaphoreType.DMA((2, 2, chunks, ring)),
        pltpu.SemaphoreType.DMA((2, 2, chunks, ring)),
        pltpu.SemaphoreType.DMA((2, 2, chunks, 7)),
        pltpu.SemaphoreType.DMA((2, chunks)),
    ]
    small = jax.ShapeDtypeStruct((2, hidden), F32)
    flat = jax.ShapeDtypeStruct((rows, hidden), BF16)
    result, grad_first, grad_weights, grad_gain, grad_shift, grad_decay = pl.pallas_call(
        functools.partial(kernel, dims),
        out_shape=(
            flat,
            flat,
            jax.ShapeDtypeStruct((2, padded, width), F32),
            small,
            small,
            small,
        ),
        in_specs=[
            vmem,
            anywhere,
            vmem,
            vmem,
            vmem,
            pl.BlockSpec(memory_space=pltpu.SMEM),
            vmem,
        ],
        out_specs=(vmem, vmem, anywhere, vmem, vmem, vmem),
        scratch_shapes=scratch,
        compiler_params=pltpu.CompilerParams(
            collective_id=0, has_side_effects=True, vmem_limit_bytes=60 << 20
        ),
    )(
        frames.reshape(rows, hidden),
        weights,
        norm_gain,
        norm_shift,
        decays,
        lengths,
        cotangent.reshape(rows, hidden),
    )
    grad_weights = grad_weights[:, :hidden, :hidden]
    return (
        result.reshape(frames.shape),
        grad_first.reshape(frames.shape),
        grad_weights,
        grad_gain,
        grad_shift,
        grad_decay,
    )


def solution(mesh):
    everywhere = P(("dp", "rep"), None, None, None)
    return jax.shard_map(
        functools.partial(body, mesh.shape["dp"] // 2),
        mesh=mesh,
        in_specs=(everywhere, P(), P(), P(), P(), P(("dp", "rep")), everywhere),
        out_specs=(everywhere, everywhere, P(), P(), P(), P()),
        check_vma=False,
    )
```

```python
import functools

import jax
import jax.numpy as jnp
from jax import lax
from jax.experimental import pallas as pl
from jax.experimental.pallas import tpu as pltpu
from jax.sharding import PartitionSpec as P

EPS = 1e-05
MESH = pl.DeviceIdType.MESH
F32 = jnp.float32
BF16 = jnp.bfloat16
LAGS = (0.88, 0.75, 1.41, 1.66, 2.89)
EXTRA = (0.61, 1.4, 2.39)
LANES = 128


def round_up(value, unit):
    return -(-value // unit) * unit


def chunk_plan(hidden, ring, step):
    plan, start = [], 0
    while start < hidden:
        span = min(step, round_up(hidden - start, 8 * ring))
        plan.append((start, span))
        start += span
    return tuple(plan), start


def ring_levels(ring):
    inner = min(4, ring)
    levels = [(1, inner, 0)]
    if ring > inner:
        levels.append((inner, ring // inner, inner))
    return tuple(levels)


def kernel(
    dims,
    frames,
    weights,
    gain,
    shift,
    decay,
    lengths,
    cotangent,
    output,
    grad_frames,
    grad_weights,
    grad_gain,
    grad_shift,
    grad_decay,
    wbuf,
    x0f,
    xb,
    ob,
    xs,
    xo,
    ys,
    yo,
    normed,
    states,
    gy,
    gpf,
    gpb,
    gr,
    xchunk,
    gb,
    dw,
    rb,
    params,
    coef,
    eight_f,
    eight_b,
    ring_f,
    ring_b,
    total_f,
    total_b,
    sem_w,
    sem_io,
    sem_x,
    sem_c,
    sem_y,
    sem_g,
    sem_e,
    sem_r,
    sem_rs,
    sem_az,
    sem_ag,
    sem_l,
):
    ring, plan, _, _, views, slots, hidden, width = dims
    chunks = len(plan)
    rows = views * slots
    piece_at = width // 8
    own_width = width // 8
    levels = ring_levels(ring)
    x1 = gpf.at[0]
    bits = ring.bit_length() - 1
    tile = 512
    blocks = slots // 8
    lane_steps = width // LANES

    dp, rep = lax.axis_index("dp"), lax.axis_index("rep")
    a, bx = dp // 2, dp % 2
    by, c = rep // 2, rep % 2
    nx, ny, nc = 1 - bx, 1 - by, 1 - c

    def device(a_at, x_at, y_at, c_at):
        return (a_at * 2 + x_at, y_at * 2 + c_at)

    core_peer = device(a, bx, by, nc)
    x_peer = device(a, nx, by, c)
    y_peer = device(a, bx, ny, c)

    def group_peer(flips):
        fx, fy, fc = flips // 4, flips // 2 % 2, flips % 2
        x_at, y_at, c_at = (nx if fx else bx), (ny if fy else by), (nc if fc else c)
        return device(a, x_at, y_at, c_at), x_at * 4 + y_at * 2 + c_at

    def ring_peer(level, step):
        stride, size, _ = levels[level]
        at = a // stride % size
        to = lax.rem(at + step, size)
        return device(a + (to - at) * stride, bx, by, c), at, to

    def each_ring(level, act):
        for step in range(1, levels[level][1]):
            act(step)

    def remote(src, dst, sems, at, target):
        return pltpu.make_async_remote_copy(
            src_ref=src,
            dst_ref=dst,
            send_sem=sems.at[(0,) + at],
            recv_sem=sems.at[(1,) + at],
            device_id=target,
            device_id_type=MESH,
        )

    barrier = pltpu.get_barrier_semaphore()
    for flips in range(1, 8):
        pl.semaphore_signal(barrier, 1, device_id=group_peer(flips)[0], device_id_type=MESH)
    for level in range(len(levels)):
        each_ring(
            level,
            lambda step: pl.semaphore_signal(
                barrier, 1, device_id=ring_peer(level, step)[0], device_id_type=MESH
            ),
        )

    def load_weight(layer, at):
        return pltpu.make_async_copy(weights.at[layer], wbuf, sem_w.at[at])

    frames_in = pltpu.make_async_copy(frames, xb, sem_io.at[0])
    frames_in.start()
    load_weight(0, 0).start()
    cotangent_in = pltpu.make_async_copy(cotangent, ob, sem_io.at[1])
    cotangent_in.start()

    length = lengths[0]
    tail = hidden - hidden % LANES
    x0f[:, tail:width] = jnp.broadcast_to(length.astype(F32), (rows, width - tail))
    gy[:, tail:width] = jnp.zeros((rows, width - tail), F32)
    frames_in.wait()
    x0f[:, :hidden] = xb[...].astype(F32)
    params[...] = jnp.zeros(params.shape, F32)
    for at, source in enumerate((gain, shift, decay)):
        params[at * 2 : at * 2 + 2, :hidden] = source[...]
    pl.semaphore_wait(barrier, 7 + sum(size - 1 for _, size, _ in levels))

    def piece(k):
        return slice(k * piece_at, (k + 1) * piece_at)

    def x_copy(k, kind):
        if kind == 3:
            source, target = (xs.at[0], y_peer) if k % 2 == 0 else (xs.at[1], x_peer)
            landing = xs.at[2]
        else:
            source = x0f
            landing, target = ((xs.at[0], x_peer), (xs.at[1], y_peer), (xo.at[0], core_peer))[kind]
        return remote(source.at[:, piece(k)], landing.at[:, piece(k)], sem_x, (k, kind), target)

    def send_x(first, last):
        for k in range(first, last):
            for kind in range(3):
                x_copy(k, kind).start()

    def send_diagonal(first, last):
        for k in range(first, last):
            x_copy(k, k % 2).wait_recv()
            x_copy(k, 3).start()

    def core_copy(at):
        return remote(xs.at[at], xo.at[at + 1], sem_c, (at,), core_peer)

    def wait_x(at):
        for k in range(8):
            if at == 2:
                x_copy(k, 3).wait_recv()
            elif k % 2 != at:
                x_copy(k, at).wait_recv()
        core_copy(at).start()

    def y_copy(at):
        return remote(ys.at[at], yo.at[at], sem_y, (at,), core_peer)

    row_at = lax.broadcasted_iota(jnp.int32, (8, LANES), 0)
    def lanes_of(step):
        return pl.ds(pl.multiple_of(step * LANES, LANES), LANES)

    def over_lanes(act):
        def go(step, _):
            act(lanes_of(step), step)
            return 0

        lax.fori_loop(0, lane_steps, go, 0)

    def valid_at(block, limit=None):
        return (row_at + block * 8).astype(F32) < (length.astype(F32) if limit is None else limit)

    def spread(row):
        return jnp.broadcast_to(row, (8, LANES))

    def row_powers(decay_row, reverse):
        one = spread(decay_row)
        two = one * one
        four = two * two
        from_edge = 7 - row_at if reverse else row_at
        ones = jnp.ones((8, LANES), F32)
        power = (
            one
            * jnp.where(from_edge % 2 == 1, one, ones)
            * jnp.where(from_edge // 2 % 2 == 1, two, ones)
            * jnp.where(from_edge // 4 == 1, four, ones)
        )
        zero = jnp.zeros((8, LANES), F32)
        return (
            jnp.where(from_edge >= 1, one, zero),
            jnp.where(from_edge >= 2, two, zero),
            jnp.where(from_edge >= 4, four, zero),
            power,
        )

    def scan_blocks(values, powers, reverse):
        one, two, four, power = powers
        count = len(values)
        order = range(count - 1, -1, -1) if reverse else range(count)
        result = [None] * count
        carry = None
        for at in order:
            value = values[at]
            for amount, factor in ((1, one), (2, two), (4, four)):
                value = value + factor * pltpu.roll(value, 8 - amount if reverse else amount, 0)
            if carry is not None:
                value = value + power * carry
            carry = spread(value[0:1] if reverse else value[7:8])
            result[at] = value
        return result

    def project(source, result):
        for at in range(0, hidden, tile):
            span = min(tile, hidden - at)
            result[:, at : at + span] = jnp.dot(
                source[...], wbuf[:, at : at + span], preferred_element_type=F32
            )
        if tail < hidden:
            kept = result[:, tail:width]
            lane = lax.broadcasted_iota(jnp.int32, kept.shape, 1)
            result[:, tail:width] = jnp.where(lane < hidden - tail, kept, 0.0)

    mine = bx * 4 + by * 2 + c

    def moments(layer):
        frame_count = (views * length).astype(F32)

        def act(lanes, step):
            first = jnp.zeros((8, LANES), F32)
            square = jnp.zeros((8, LANES), F32)
            for view in range(views):
                for block in range(blocks):
                    value = normed[layer, view * slots + block * 8 : view * slots + block * 8 + 8, lanes]
                    value = jnp.where(valid_at(block), value, 0.0)
                    first += value
                    square += value * value
            first = jnp.sum(first, axis=0, keepdims=True)
            lane = lax.broadcasted_iota(jnp.int32, (1, LANES), 1) + step * LANES
            first = jnp.where(lane >= hidden, frame_count, first)
            eight_f[layer, mine, 0:1, lanes] = first
            eight_f[layer, mine, 1:2, lanes] = jnp.sum(square, axis=0, keepdims=True)

        over_lanes(act)

    def start_sum(eight, at):
        for flips in range(1, 8):
            peer, _ = group_peer(flips)
            remote(eight.at[mine], eight.at[mine], sem_e, (at, flips - 1), peer).start()

    def ring_copy(around, at, level, step, slot):
        _, _, first = levels[level]
        peer, _, _ = ring_peer(level, step)
        ref = around.at[first + slot]
        return remote(ref, ref, sem_r, (at, first + step), peer)

    def ring_send(around, at, level, total):
        _, _, first = levels[level]
        _, own, _ = ring_peer(level, 1)
        around[first + own] = total
        each_ring(level, lambda step: ring_copy(around, at, level, step, own).start())

    def middle_sum(eight, around, at):
        for flips in range(1, 8):
            peer, slot = group_peer(flips)
            remote(eight.at[mine], eight.at[slot], sem_e, (at, flips - 1), peer).wait_recv()
        total = eight[0]
        for slot in range(1, 8):
            total = total + eight[slot]
        ring_send(around, at, 0, total)

    def finish_sum(eight, around, at, result):
        for level, (stride, size, first) in enumerate(levels):

            def wait(step):
                behind = lax.rem(a // stride % size + size - step, size)
                ring_copy(around, at, level, step, behind).wait_recv()

            each_ring(level, wait)
            total = around[first]
            for slot in range(1, size):
                total = total + around[first + slot]
            if level + 1 < len(levels):
                ring_send(around, at, level + 1, total)
        result[...] = total

    def statistics(layer, lanes):
        count = jnp.broadcast_to(total_f[layer, 0:1, width - 1 : width], (1, LANES))
        average = total_f[layer, 0:1, lanes] / count
        variance = total_f[layer, 1:2, lanes] / count - average * average
        return average, lax.rsqrt(variance + EPS), count

    def forward(layer):
        def act(lanes, step):
            average, inverse, _ = statistics(layer, lanes)
            coef[layer : layer + 1, lanes] = inverse
            average, inverse = spread(average), spread(inverse)
            gain_row = spread(params[layer : layer + 1, lanes])
            shift_row = spread(params[2 + layer : 3 + layer, lanes])
            powers = row_powers(params[4 + layer : 5 + layer, lanes], False)
            for view in range(views):
                drives = []
                for block in range(blocks):
                    at = view * slots + block * 8
                    value = (normed[layer, at : at + 8, lanes] - average) * inverse
                    normed[layer, at : at + 8, lanes] = value
                    drives.append(gain_row * value + shift_row)
                result = scan_blocks(drives, powers, False)
                for block in range(blocks):
                    at = view * slots + block * 8
                    state = result[block]
                    states[layer, at : at + 8, lanes] = state
                    bump = jnp.where(valid_at(block), softplus(state), 0.0)
                    if layer == 0:
                        following = x0f[at : at + 8, lanes] + bump
                        x1[at : at + 8, lanes] = following
                        ys[0, at : at + 8, lanes] = following.astype(BF16).astype(F32)
                    else:
                        x1[at : at + 8, lanes] = x1[at : at + 8, lanes] + bump

        over_lanes(act)

    def softplus(state):
        return jnp.maximum(state, 0.0) + jnp.log1p(jnp.exp(-jnp.abs(state)))

    def repeat_forward(at):
        xb[...] = xs[at, :, :hidden].astype(BF16)
        project(xb, ys.at[at + 1])
        limit = spread(xs[at, 0:1, width - LANES : width])
        limit = jnp.broadcast_to(limit[:, LANES - 1 :], (8, LANES))

        def act(lanes, step):
            average, inverse, _ = statistics(0, lanes)
            gain_row = spread(params[0:1, lanes] * inverse)
            shift_row = spread(params[2:3, lanes] - average * inverse * params[0:1, lanes])
            powers = row_powers(params[4:5, lanes], False)
            for view in range(views):
                drives = []
                for block in range(blocks):
                    row = view * slots + block * 8
                    drives.append(gain_row * ys[at + 1, row : row + 8, lanes] + shift_row)
                result = scan_blocks(drives, powers, False)
                for block in range(blocks):
                    row = view * slots + block * 8
                    bump = jnp.where(valid_at(block, limit), softplus(result[block]), 0.0)
                    following = xs[at, row : row + 8, lanes] + bump
                    ys[at + 1, row : row + 8, lanes] = following.astype(BF16).astype(F32)

        over_lanes(act)
        y_copy(at + 1).start()

    def backward_sums(layer):
        def act(lanes, step):
            powers = row_powers(params[4 + layer : 5 + layer, lanes], True)
            sums = [jnp.zeros((8, LANES), F32) for _ in range(3)]
            for view in range(views):
                sources = []
                kept = []
                for block in range(blocks):
                    at = view * slots + block * 8
                    state = states[layer, at : at + 8, lanes]
                    kept.append(state)
                    slope = 1.0 / (1.0 + jnp.exp(-state))
                    slope = gy[at : at + 8, lanes] * slope
                    sources.append(jnp.where(valid_at(block), slope, 0.0))
                carried = scan_blocks(sources, powers, True)
                for block in range(blocks):
                    at = view * slots + block * 8
                    value = carried[block]
                    gpf[layer, at : at + 8, lanes] = value
                    shifted = pltpu.roll(kept[block], 1, 0)
                    before = spread(kept[block - 1][7:8]) if block else jnp.zeros((8, LANES), F32)
                    shifted = jnp.where(row_at == 0, before, shifted)
                    sums[0] += value * normed[layer, at : at + 8, lanes]
                    sums[1] += value
                    sums[2] += value * shifted
            for at in range(3):
                eight_b[layer, mine, at : at + 1, lanes] = jnp.sum(sums[at], axis=0, keepdims=True)
            eight_b[layer, mine, 3:4, lanes] = jnp.zeros((1, LANES), F32)

        over_lanes(act)

    def backward_drive(layer):
        grad_gain[layer : layer + 1, :] = total_b[layer, 0:1, :hidden]
        grad_shift[layer : layer + 1, :] = total_b[layer, 1:2, :hidden]
        grad_decay[layer : layer + 1, :] = total_b[layer, 2:3, :hidden]

        def act(lanes, step):
            count = jnp.broadcast_to(total_f[layer, 0:1, width - 1 : width], (1, LANES))
            slope = spread(total_b[layer, 0:1, lanes] / count)
            offset = spread(total_b[layer, 1:2, lanes] / count)
            scale = spread(coef[layer : layer + 1, lanes] * params[layer : layer + 1, lanes])
            for view in range(views):
                for block in range(0, blocks, 2):
                    pair = []
                    for side in range(2):
                        at = view * slots + (block + side) * 8
                        drop = offset + normed[layer, at : at + 8, lanes] * slope
                        drop = jnp.where(valid_at(block + side), drop, 0.0)
                        pair.append(scale * (gpf[layer, at : at + 8, lanes] - drop))
                    at = view * slots + block * 8
                    low = jnp.concatenate(pair, axis=0).astype(BF16)
                    gpb[at : at + 16, lanes] = low
                    gpf[layer, at : at + 16, lanes] = low.astype(F32)

        over_lanes(act)

    def columns_of(slot):
        return pl.ds(pl.multiple_of(slot * own_width, own_width), own_width)

    def place(flips):
        return flips % 2 * 4 + flips // 4 + flips // 2 % 2 * 2

    def grad_copies(layer):
        result = []
        for flips in (7, 6, 5, 4, 3, 2, 1):
            peer, slot = group_peer(flips)
            result.append(
                remote(
                    gpf.at[layer, :, columns_of(slot)],
                    gr.at[layer, place(flips) - 1],
                    sem_g,
                    (layer, flips - 1),
                    peer,
                )
            )
        return result

    def back_project():
        for at in range(0, hidden, tile):
            span = min(tile, hidden - at)
            gy[:, at : at + span] += lax.dot_general(
                gpb[:, :hidden],
                wbuf[at : at + span, :],
                (((1,), (1,)), ((), ())),
                preferred_element_type=F32,
            )

    def load_factors(layer):
        for copy in grad_copies(layer):
            copy.wait_recv()
        gb[0:rows, :] = gpf[layer, :, columns_of(mine)].astype(BF16)
        for at in range(1, 8):
            gb[at * rows : (at + 1) * rows, :] = gr[layer, at - 1].astype(BF16)
        for at in range(4):
            if layer == 1:
                y_copy(at).wait_recv()
            elif at:
                core_copy(at - 1).wait_recv()
            else:
                for k in range(8):
                    x_copy(k, 2).wait_recv()

    def span_of(k):
        start, span = plan[k]
        return slice(start, start + span)

    def weight_product(layer, k):
        if k == 0:
            load_factors(layer)
        start, span = plan[k]
        for at in range(8):
            if layer == 0:
                source = x0f if at == 0 else xs.at[at - 1] if at < 4 else xo.at[at - 4]
            else:
                source = ys.at[at] if at < 4 else yo.at[at - 4]
            xchunk[at * rows : (at + 1) * rows, :span] = source[:, span_of(k)].astype(BF16)
        dw[layer, span_of(k), :] = lax.dot_general(
            xchunk[:, :span], gb[...], (((0,), (0,)), ((), ())), preferred_element_type=F32
        )
        fold_copy(layer, k, 0).start()

    def bit_of(at):
        return a // 2**at % 2

    def bit_peer(at):
        return device(a + (1 - 2 * bit_of(at)) * 2**at, bx, by, c)

    def region(k, count):
        start, span = plan[k]
        first = start
        for at in range(count):
            first = first + bit_of(at) * (span >> (at + 1))
        return first

    def rows_at(first, count):
        return pl.ds(pl.multiple_of(first, 8), count)

    def fold_copy(layer, k, at):
        start, span = plan[k]
        part = span >> (at + 1)
        source = rows_at(region(k, at) + (1 - bit_of(at)) * part, part)
        landing = start + span - (span >> at)
        return remote(
            dw.at[layer, source],
            rb.at[layer, slice(landing, landing + part)],
            sem_rs,
            (layer, k, at),
            bit_peer(at),
        )

    def fold(layer, k, at):
        fold_copy(layer, k, at).wait_recv()
        start, span = plan[k]
        part = span >> (at + 1)
        landing = start + span - (span >> at)
        kept = rows_at(region(k, at + 1), part)
        dw[layer, kept, :] = dw[layer, kept, :] + rb[layer, landing : landing + part, :]
        if at + 1 < bits:
            fold_copy(layer, k, at + 1).start()
        else:
            local_copy(layer, k).start()
            widen_copy(layer, k, at).start()

    def local_copy(layer, k):
        kept = rows_at(region(k, bits), plan[k][1] >> bits)
        return pltpu.make_async_copy(
            dw.at[layer, kept], grad_weights.at[layer, kept, columns_of(mine)], sem_l.at[layer, k]
        )

    def widen_copy(layer, k, at):
        held = rows_at(region(k, at + 1), plan[k][1] >> (at + 1))
        landing = grad_weights.at[layer, held, columns_of(mine)]
        source = dw.at[layer, held] if at + 1 == bits else landing
        return remote(source, landing, sem_az, (layer, k, at), bit_peer(at))

    def widen(layer, k, at):
        part = plan[k][1] >> (at + 1)
        other = rows_at(region(k, at) + (1 - bit_of(at)) * part, part)
        landing = grad_weights.at[layer, other, columns_of(mine)]
        remote(landing, landing, sem_az, (layer, k, at), bit_peer(at)).wait_recv()
        if at + 1 == bits:
            local_copy(layer, k).wait()
        if at:
            widen_copy(layer, k, at - 1).start()
        else:
            for kind in (0, 1, 3):
                block_copy(layer, k, kind).start()

    def order_of(layer, k):
        own, flip_x = (bx, by), (nx, by)
        flip_y, both = (bx, ny), (nx, ny)
        if (k + layer) % 2 == 1:
            return (own, flip_x, flip_y, both), x_peer, y_peer
        return (own, flip_y, flip_x, both), y_peer, x_peer

    def block(layer, k, x_at, y_at, c_at):
        return grad_weights.at[layer, span_of(k), columns_of(x_at * 4 + y_at * 2 + c_at)]

    def block_copy(layer, k, kind):
        spots, first, second = order_of(layer, k)
        spot, peer = {
            0: (0, first),
            1: (0, second),
            2: (1, second),
            3: (0, core_peer),
            4: (1, core_peer),
            5: (2, core_peer),
            6: (3, core_peer),
        }[kind]
        held = block(layer, k, *spots[spot], c)
        return remote(held, held, sem_ag, (layer, k, kind), peer)

    def arrived(layer, k, kind):
        spots, first, second = order_of(layer, k)
        spot = {0: 1, 1: 2, 2: 3, 3: 0, 4: 1, 5: 2, 6: 3}[kind]
        landing = block(layer, k, *spots[spot], nc if kind >= 3 else c)
        remote(landing, landing, sem_ag, (layer, k, kind), core_peer).wait_recv()

    def gather(layer, k, at):
        arrived(layer, k, at)
        if at == 0:
            block_copy(layer, k, 2).start()
        block_copy(layer, k, 4 + at).start()

    def write_out(target, value, at):
        ob[...] = value
        copy = pltpu.make_async_copy(ob, target, sem_io.at[at])
        copy.start()
        return copy

    send_x(0, 1)
    load_weight(0, 0).wait()
    project(xb, normed.at[0])
    load_weight(1, 1).start()
    moments(0)
    start_sum(eight_f.at[0], 0)
    send_x(1, 4)
    cotangent_in.wait()
    gy[:, :hidden] = ob[...].astype(F32)
    middle_sum(eight_f.at[0], ring_f.at[0], 0)
    finish_sum(eight_f.at[0], ring_f.at[0], 0, total_f.at[0])
    forward(0)
    y_copy(0).start()
    xb[...] = ys[0, :, :hidden].astype(BF16)
    load_weight(1, 1).wait()
    project(xb, normed.at[1])
    moments(1)
    start_sum(eight_f.at[1], 1)
    send_x(4, 7)
    middle_sum(eight_f.at[1], ring_f.at[1], 1)
    finish_sum(eight_f.at[1], ring_f.at[1], 1, total_f.at[1])
    forward(1)
    backward_sums(1)
    start_sum(eight_b.at[1], 2)
    send_x(7, 8)
    send_diagonal(0, 2)
    result_out = write_out(output, x1[:, :hidden].astype(BF16), 2)
    middle_sum(eight_b.at[1], ring_b.at[1], 2)
    finish_sum(eight_b.at[1], ring_b.at[1], 2, total_b.at[1])
    backward_drive(1)
    send_diagonal(2, 8)
    for copy in grad_copies(1):
        copy.start()
    back_project()
    load_weight(0, 2).start()
    backward_sums(0)
    start_sum(eight_b.at[0], 3)
    wait_x(0)
    wait_x(1)
    load_weight(0, 2).wait()
    repeat_forward(0)
    repeat_forward(1)
    wait_x(2)
    repeat_forward(2)

    def finish_backward(layer, k):
        finish_sum(eight_b.at[0], ring_b.at[0], 3, total_b.at[0])
        backward_drive(0)
        for copy in grad_copies(0):
            copy.start()

    def finish_input(layer, k):
        back_project()
        result_out.wait()
        write_out(grad_frames, gy[:, :hidden].astype(BF16), 3)

    stages = [(weight_product, 0.0)]
    for at in range(bits):
        stages.append((functools.partial(fold, at=at), LAGS[0] * (at + 1)))
    for at in range(bits):
        stages.append(
            (functools.partial(widen, at=bits - 1 - at), LAGS[0] * bits + LAGS[1] * (at + 1))
        )
    for at in range(3):
        stages.append(
            (functools.partial(gather, at=at), LAGS[0] * bits + LAGS[1] * bits + LAGS[2 + at])
        )
    tasks = [
        (EXTRA[0], 0, 0, 0, lambda layer, k: middle_sum(eight_b.at[0], ring_b.at[0], 3)),
        (EXTRA[1], 0, 0, 0, finish_backward),
        (EXTRA[2], 0, 0, 0, finish_input),
    ]
    for layer in (1, 0):
        for k in range(chunks):
            for at, (stage, lag) in enumerate(stages):
                tasks.append(((1 - layer) * chunks + k + lag, -at, layer, k, stage))
    tasks.sort(key=lambda task: task[:2])
    for _, _, layer, k, stage in tasks:
        stage(layer, k)

    pltpu.make_async_copy(ob, grad_frames, sem_io.at[3]).wait()
    for k in range(8):
        for kind in range(4):
            x_copy(k, kind).wait_send()
    for at in range(3):
        core_copy(at).wait_send()
    for at in range(4):
        y_copy(at).wait_send()
    for layer in (1, 0):
        for copy in grad_copies(layer):
            copy.wait_send()
        for k in range(chunks):
            for at in range(bits):
                fold_copy(layer, k, at).wait_send()
                widen_copy(layer, k, at).wait_send()
            for kind in range(7):
                block_copy(layer, k, kind).wait_send()
            for kind in range(3, 7):
                arrived(layer, k, kind)
    for at, eight, around in (
        (0, eight_f.at[0], ring_f.at[0]),
        (1, eight_f.at[1], ring_f.at[1]),
        (2, eight_b.at[1], ring_b.at[1]),
        (3, eight_b.at[0], ring_b.at[0]),
    ):
        for flips in range(1, 8):
            peer, _ = group_peer(flips)
            remote(eight.at[mine], eight.at[mine], sem_e, (at, flips - 1), peer).wait_send()
        for level in range(len(levels)):
            _, own, _ = ring_peer(level, 1)
            each_ring(level, lambda step: ring_copy(around, at, level, step, own).wait_send())


def body(ring, frames, weights, norm_gain, norm_shift, decays, lengths, cotangent):
    _, views, slots, hidden = frames.shape
    width = round_up(hidden, 4 * LANES)
    rows = views * slots
    step_rows = width // 8
    own_width = width // 8
    plan, padded = chunk_plan(hidden, ring, step_rows)
    chunks = len(plan)
    dims = (ring, plan, padded, step_rows, views, slots, hidden, width)
    bits = ring.bit_length() - 1
    around = sum(size for _, size, _ in ring_levels(ring))
    vmem = pl.BlockSpec(memory_space=pltpu.VMEM)
    anywhere = pl.BlockSpec(memory_space=pl.ANY)
    scratch = [
        pltpu.VMEM((hidden, hidden), BF16),
        pltpu.VMEM((rows, width), F32),
        pltpu.VMEM((rows, hidden), BF16),
        pltpu.VMEM((rows, hidden), BF16),
        pltpu.VMEM((3, rows, width), F32),
        pltpu.VMEM((4, rows, width), F32),
        pltpu.VMEM((4, rows, width), F32),
        pltpu.VMEM((4, rows, width), F32),
        pltpu.VMEM((2, rows, width), F32),
        pltpu.VMEM((2, rows, width), F32),
        pltpu.VMEM((rows, width), F32),
        pltpu.VMEM((2, rows, width), F32),
        pltpu.VMEM((rows, width), BF16),
        pltpu.VMEM((2, 7, rows, own_width), F32),
        pltpu.VMEM((8 * rows, step_rows), BF16),
        pltpu.VMEM((8 * rows, own_width), BF16),
        pltpu.VMEM((2, padded, own_width), F32),
        pltpu.VMEM((2, padded, own_width), F32),
        pltpu.VMEM((8, width), F32),
        pltpu.VMEM((2, width), F32),
        pltpu.VMEM((2, 8, 2, width), F32),
        pltpu.VMEM((2, 8, 4, width), F32),
        pltpu.VMEM((2, around, 2, width), F32),
        pltpu.VMEM((2, around, 4, width), F32),
        pltpu.VMEM((2, 2, width), F32),
        pltpu.VMEM((2, 4, width), F32),
        pltpu.SemaphoreType.DMA((3,)),
        pltpu.SemaphoreType.DMA((4,)),
        pltpu.SemaphoreType.DMA((2, 8, 4)),
        pltpu.SemaphoreType.DMA((2, 3)),
        pltpu.SemaphoreType.DMA((2, 4)),
        pltpu.SemaphoreType.DMA((2, 2, 7)),
        pltpu.SemaphoreType.DMA((2, 4, 7)),
        pltpu.SemaphoreType.DMA((2, 4, around)),
        pltpu.SemaphoreType.DMA((2, 2, chunks, bits)),
        pltpu.SemaphoreType.DMA((2, 2, chunks, bits)),
        pltpu.SemaphoreType.DMA((2, 2, chunks, 7)),
        pltpu.SemaphoreType.DMA((2, chunks)),
    ]
    small = jax.ShapeDtypeStruct((2, hidden), F32)
    flat = jax.ShapeDtypeStruct((rows, hidden), BF16)
    result, grad_first, grad_weights, grad_gain, grad_shift, grad_decay = pl.pallas_call(
        functools.partial(kernel, dims),
        out_shape=(
            flat,
            flat,
            jax.ShapeDtypeStruct((2, padded, width), F32),
            small,
            small,
            small,
        ),
        in_specs=[
            anywhere,
            anywhere,
            vmem,
            vmem,
            vmem,
            pl.BlockSpec(memory_space=pltpu.SMEM),
            anywhere,
        ],
        out_specs=(anywhere, anywhere, anywhere, vmem, vmem, vmem),
        scratch_shapes=scratch,
        compiler_params=pltpu.CompilerParams(
            collective_id=0, has_side_effects=True, vmem_limit_bytes=60 << 20
        ),
    )(
        frames.reshape(rows, hidden),
        weights,
        norm_gain,
        norm_shift,
        decays,
        lengths,
        cotangent.reshape(rows, hidden),
    )
    grad_weights = grad_weights[:, :hidden, :hidden]
    return (
        result.reshape(frames.shape),
        grad_first.reshape(frames.shape),
        grad_weights,
        grad_gain,
        grad_shift,
        grad_decay,
    )


def solution(mesh):
    everywhere = P(("dp", "rep"), None, None, None)
    return jax.shard_map(
        functools.partial(body, mesh.shape["dp"] // 2),
        mesh=mesh,
        in_specs=(everywhere, P(), P(), P(), P(), P(("dp", "rep")), everywhere),
        out_specs=(everywhere, everywhere, P(), P(), P(), P()),
        check_vma=False,
    )
```

```python
import functools

import jax
import jax.numpy as jnp
from jax import lax
from jax.experimental import pallas as pl
from jax.experimental.pallas import tpu as pltpu
from jax.sharding import PartitionSpec as P

EPS = 1e-05
MESH = pl.DeviceIdType.MESH
F32 = jnp.float32
BF16 = jnp.bfloat16
LAGS = (1.06, 0.71, 1.63, 1.73, 4.42)
SUM_DUE = 0.43
DRIVE_DUE = 1.4
INPUT_DUE = 2.4
SHARE = 0.72
STEPS = 16
LANES = 128


def round_up(value, unit):
    return -(-value // unit) * unit


def chunk_plan(hidden, ring, step):
    plan, start = [], 0
    while start < hidden:
        span = min(step, round_up(hidden - start, 8 * ring))
        plan.append((start, span))
        start += span
    return tuple(plan), start


def ring_levels(ring):
    inner = min(4, ring)
    levels = [(1, inner, 0)]
    if ring > inner:
        levels.append((inner, ring // inner, inner))
    return tuple(levels)


def kernel(
    dims,
    frames,
    weights,
    gain,
    shift,
    decay,
    lengths,
    cotangent,
    output,
    grad_frames,
    grad_weights,
    grad_gain,
    grad_shift,
    grad_decay,
    wbuf,
    x0f,
    xb,
    ob,
    xs,
    xo,
    ys,
    yo,
    normed,
    states,
    gy,
    gpf,
    gpb,
    gr,
    xchunk,
    gb,
    dw,
    rb,
    params,
    coef,
    eight_f,
    eight_b,
    ring_f,
    ring_b,
    total_f,
    total_b,
    sem_w,
    sem_io,
    sem_x,
    sem_c,
    sem_y,
    sem_g,
    sem_e,
    sem_r,
    sem_rs,
    sem_az,
    sem_ag,
    sem_l,
):
    ring, plan, padded, _, views, slots, hidden, width = dims
    chunks = len(plan)
    rows = views * slots
    piece_at = width // 8
    own_width = width // 8
    levels = ring_levels(ring)
    x1 = gpf.at[0]
    bits = ring.bit_length() - 1
    tile = 512
    blocks = slots // 8
    lane_steps = width // LANES

    dp, rep = lax.axis_index("dp"), lax.axis_index("rep")
    a, bx = dp // 2, dp % 2
    by, c = rep // 2, rep % 2
    nx, ny, nc = 1 - bx, 1 - by, 1 - c

    def device(a_at, x_at, y_at, c_at):
        return (a_at * 2 + x_at, y_at * 2 + c_at)

    core_peer = device(a, bx, by, nc)
    x_peer = device(a, nx, by, c)
    y_peer = device(a, bx, ny, c)

    def group_peer(flips):
        fx, fy, fc = flips // 4, flips // 2 % 2, flips % 2
        x_at, y_at, c_at = (nx if fx else bx), (ny if fy else by), (nc if fc else c)
        return device(a, x_at, y_at, c_at), x_at * 4 + y_at * 2 + c_at

    def ring_peer(level, step):
        stride, size, _ = levels[level]
        at = a // stride % size
        to = lax.rem(at + step, size)
        return device(a + (to - at) * stride, bx, by, c), at, to

    def each_ring(level, act):
        for step in range(1, levels[level][1]):
            act(step)

    def remote(src, dst, sems, at, target):
        return pltpu.make_async_remote_copy(
            src_ref=src,
            dst_ref=dst,
            send_sem=sems.at[(0,) + at],
            recv_sem=sems.at[(1,) + at],
            device_id=target,
            device_id_type=MESH,
        )

    barrier = pltpu.get_barrier_semaphore()
    for flips in range(1, 8):
        pl.semaphore_signal(barrier, 1, device_id=group_peer(flips)[0], device_id_type=MESH)
    for level in range(len(levels)):
        each_ring(
            level,
            lambda step: pl.semaphore_signal(
                barrier, 1, device_id=ring_peer(level, step)[0], device_id_type=MESH
            ),
        )

    def load_weight(layer, at):
        return pltpu.make_async_copy(weights.at[layer], wbuf, sem_w.at[at])

    frames_in = pltpu.make_async_copy(frames, xb, sem_io.at[0])
    frames_in.start()
    load_weight(0, 0).start()
    cotangent_in = pltpu.make_async_copy(cotangent, ob, sem_io.at[1])
    cotangent_in.start()

    length = lengths[0]
    tail = hidden - hidden % LANES
    x0f[:, tail:width] = jnp.broadcast_to(length.astype(F32), (rows, width - tail))
    gy[:, tail:width] = jnp.zeros((rows, width - tail), F32)
    frames_in.wait()
    x0f[:, :hidden] = xb[...].astype(F32)
    params[...] = jnp.zeros(params.shape, F32)
    for at, source in enumerate((gain, shift, decay)):
        params[at * 2 : at * 2 + 2, :hidden] = source[...]
    pl.semaphore_wait(barrier, 7 + sum(size - 1 for _, size, _ in levels))

    def piece(k):
        return slice(k * piece_at, (k + 1) * piece_at)

    def x_copy(k, kind):
        if kind == 3:
            source, target = (xs.at[0], y_peer) if k % 2 == 0 else (xs.at[1], x_peer)
            landing = xs.at[2]
        else:
            source = x0f
            landing, target = ((xs.at[0], x_peer), (xs.at[1], y_peer), (xo.at[0], core_peer))[kind]
        return remote(source.at[:, piece(k)], landing.at[:, piece(k)], sem_x, (k, kind), target)

    def send_x(first, last):
        for k in range(first, last):
            for kind in range(3):
                x_copy(k, kind).start()

    def send_diagonal(first, last):
        for k in range(first, last):
            x_copy(k, k % 2).wait_recv()
            x_copy(k, 3).start()

    def core_copy(at):
        return remote(xs.at[at], xo.at[at + 1], sem_c, (at,), core_peer)

    def wait_x(at):
        for k in range(8):
            if at == 2:
                x_copy(k, 3).wait_recv()
            elif k % 2 != at:
                x_copy(k, at).wait_recv()
        core_copy(at).start()

    def y_copy(at):
        return remote(ys.at[at], yo.at[at], sem_y, (at,), core_peer)

    row_at = lax.broadcasted_iota(jnp.int32, (8, LANES), 0)
    def lanes_of(step):
        return pl.ds(pl.multiple_of(step * LANES, LANES), LANES)

    def over_lanes(act):
        def go(step, _):
            act(lanes_of(step), step)
            return 0

        lax.fori_loop(0, lane_steps, go, 0)

    def valid_at(block, limit=None):
        return (row_at + block * 8).astype(F32) < (length.astype(F32) if limit is None else limit)

    def spread(row):
        return jnp.broadcast_to(row, (8, LANES))

    def row_powers(decay_row, reverse):
        one = spread(decay_row)
        two = one * one
        four = two * two
        from_edge = 7 - row_at if reverse else row_at
        ones = jnp.ones((8, LANES), F32)
        power = (
            one
            * jnp.where(from_edge % 2 == 1, one, ones)
            * jnp.where(from_edge // 2 % 2 == 1, two, ones)
            * jnp.where(from_edge // 4 == 1, four, ones)
        )
        zero = jnp.zeros((8, LANES), F32)
        return (
            jnp.where(from_edge >= 1, one, zero),
            jnp.where(from_edge >= 2, two, zero),
            jnp.where(from_edge >= 4, four, zero),
            power,
        )

    def scan_blocks(values, powers, reverse):
        one, two, four, power = powers
        count = len(values)
        order = range(count - 1, -1, -1) if reverse else range(count)
        result = [None] * count
        carry = None
        for at in order:
            value = values[at]
            for amount, factor in ((1, one), (2, two), (4, four)):
                value = value + factor * pltpu.roll(value, 8 - amount if reverse else amount, 0)
            if carry is not None:
                value = value + power * carry
            carry = spread(value[0:1] if reverse else value[7:8])
            result[at] = value
        return result

    def project(source, result):
        for at in range(0, hidden, tile):
            span = min(tile, hidden - at)
            result[:, at : at + span] = jnp.dot(
                source[...], wbuf[:, at : at + span], preferred_element_type=F32
            )
        if tail < hidden:
            kept = result[:, tail:width]
            lane = lax.broadcasted_iota(jnp.int32, kept.shape, 1)
            result[:, tail:width] = jnp.where(lane < hidden - tail, kept, 0.0)

    mine = bx * 4 + by * 2 + c

    def moments(layer):
        frame_count = (views * length).astype(F32)

        def act(lanes, step):
            first = jnp.zeros((8, LANES), F32)
            square = jnp.zeros((8, LANES), F32)
            for view in range(views):
                for block in range(blocks):
                    value = normed[layer, view * slots + block * 8 : view * slots + block * 8 + 8, lanes]
                    value = jnp.where(valid_at(block), value, 0.0)
                    first += value
                    square += value * value
            first = jnp.sum(first, axis=0, keepdims=True)
            lane = lax.broadcasted_iota(jnp.int32, (1, LANES), 1) + step * LANES
            first = jnp.where(lane >= hidden, frame_count, first)
            eight_f[layer, mine, 0:1, lanes] = first
            eight_f[layer, mine, 1:2, lanes] = jnp.sum(square, axis=0, keepdims=True)

        over_lanes(act)

    def start_sum(eight, at):
        for flips in range(1, 8):
            peer, _ = group_peer(flips)
            remote(eight.at[mine], eight.at[mine], sem_e, (at, flips - 1), peer).start()

    def ring_copy(around, at, level, step, slot):
        _, _, first = levels[level]
        peer, _, _ = ring_peer(level, step)
        ref = around.at[first + slot]
        return remote(ref, ref, sem_r, (at, first + step), peer)

    def ring_send(around, at, level, total):
        _, _, first = levels[level]
        _, own, _ = ring_peer(level, 1)
        around[first + own] = total
        each_ring(level, lambda step: ring_copy(around, at, level, step, own).start())

    def middle_sum(eight, around, at):
        for flips in range(1, 8):
            peer, slot = group_peer(flips)
            remote(eight.at[mine], eight.at[slot], sem_e, (at, flips - 1), peer).wait_recv()
        total = eight[0]
        for slot in range(1, 8):
            total = total + eight[slot]
        ring_send(around, at, 0, total)

    def finish_sum(eight, around, at, result):
        for level, (stride, size, first) in enumerate(levels):

            def wait(step):
                behind = lax.rem(a // stride % size + size - step, size)
                ring_copy(around, at, level, step, behind).wait_recv()

            each_ring(level, wait)
            total = around[first]
            for slot in range(1, size):
                total = total + around[first + slot]
            if level + 1 < len(levels):
                ring_send(around, at, level + 1, total)
        result[...] = total

    def statistics(layer, lanes):
        count = jnp.broadcast_to(total_f[layer, 0:1, width - 1 : width], (1, LANES))
        average = total_f[layer, 0:1, lanes] / count
        variance = total_f[layer, 1:2, lanes] / count - average * average
        return average, lax.rsqrt(variance + EPS), count

    def forward(layer):
        def act(lanes, step):
            average, inverse, _ = statistics(layer, lanes)
            coef[layer : layer + 1, lanes] = inverse
            average, inverse = spread(average), spread(inverse)
            gain_row = spread(params[layer : layer + 1, lanes])
            shift_row = spread(params[2 + layer : 3 + layer, lanes])
            powers = row_powers(params[4 + layer : 5 + layer, lanes], False)
            for view in range(views):
                drives = []
                for block in range(blocks):
                    at = view * slots + block * 8
                    value = (normed[layer, at : at + 8, lanes] - average) * inverse
                    normed[layer, at : at + 8, lanes] = value
                    drives.append(gain_row * value + shift_row)
                result = scan_blocks(drives, powers, False)
                for block in range(blocks):
                    at = view * slots + block * 8
                    state = result[block]
                    states[layer, at : at + 8, lanes] = state
                    bump = jnp.where(valid_at(block), softplus(state), 0.0)
                    if layer == 0:
                        following = x0f[at : at + 8, lanes] + bump
                        x1[at : at + 8, lanes] = following
                        ys[0, at : at + 8, lanes] = following.astype(BF16).astype(F32)
                    else:
                        x1[at : at + 8, lanes] = x1[at : at + 8, lanes] + bump

        over_lanes(act)

    def softplus(state):
        return jnp.maximum(state, 0.0) + jnp.log1p(jnp.exp(-jnp.abs(state)))

    def repeat_forward(at):
        xb[...] = xs[at, :, :hidden].astype(BF16)
        project(xb, ys.at[at + 1])
        limit = spread(xs[at, 0:1, width - LANES : width])
        limit = jnp.broadcast_to(limit[:, LANES - 1 :], (8, LANES))

        def act(lanes, step):
            average, inverse, _ = statistics(0, lanes)
            gain_row = spread(params[0:1, lanes] * inverse)
            shift_row = spread(params[2:3, lanes] - average * inverse * params[0:1, lanes])
            powers = row_powers(params[4:5, lanes], False)
            for view in range(views):
                drives = []
                for block in range(blocks):
                    row = view * slots + block * 8
                    drives.append(gain_row * ys[at + 1, row : row + 8, lanes] + shift_row)
                result = scan_blocks(drives, powers, False)
                for block in range(blocks):
                    row = view * slots + block * 8
                    bump = jnp.where(valid_at(block, limit), softplus(result[block]), 0.0)
                    following = xs[at, row : row + 8, lanes] + bump
                    ys[at + 1, row : row + 8, lanes] = following.astype(BF16).astype(F32)

        over_lanes(act)
        y_copy(at + 1).start()

    def backward_sums(layer):
        def act(lanes, step):
            powers = row_powers(params[4 + layer : 5 + layer, lanes], True)
            sums = [jnp.zeros((8, LANES), F32) for _ in range(3)]
            for view in range(views):
                sources = []
                kept = []
                for block in range(blocks):
                    at = view * slots + block * 8
                    state = states[layer, at : at + 8, lanes]
                    kept.append(state)
                    slope = 1.0 / (1.0 + jnp.exp(-state))
                    slope = gy[at : at + 8, lanes] * slope
                    sources.append(jnp.where(valid_at(block), slope, 0.0))
                carried = scan_blocks(sources, powers, True)
                for block in range(blocks):
                    at = view * slots + block * 8
                    value = carried[block]
                    gpf[layer, at : at + 8, lanes] = value
                    shifted = pltpu.roll(kept[block], 1, 0)
                    before = spread(kept[block - 1][7:8]) if block else jnp.zeros((8, LANES), F32)
                    shifted = jnp.where(row_at == 0, before, shifted)
                    sums[0] += value * normed[layer, at : at + 8, lanes]
                    sums[1] += value
                    sums[2] += value * shifted
            for at in range(3):
                eight_b[layer, mine, at : at + 1, lanes] = jnp.sum(sums[at], axis=0, keepdims=True)
            eight_b[layer, mine, 3:4, lanes] = jnp.zeros((1, LANES), F32)

        over_lanes(act)

    def backward_drive(layer):
        grad_gain[layer : layer + 1, :] = total_b[layer, 0:1, :hidden]
        grad_shift[layer : layer + 1, :] = total_b[layer, 1:2, :hidden]
        grad_decay[layer : layer + 1, :] = total_b[layer, 2:3, :hidden]

        def act(lanes, step):
            count = jnp.broadcast_to(total_f[layer, 0:1, width - 1 : width], (1, LANES))
            slope = spread(total_b[layer, 0:1, lanes] / count)
            offset = spread(total_b[layer, 1:2, lanes] / count)
            scale = spread(coef[layer : layer + 1, lanes] * params[layer : layer + 1, lanes])
            for view in range(views):
                for block in range(0, blocks, 2):
                    pair = []
                    for side in range(2):
                        at = view * slots + (block + side) * 8
                        drop = offset + normed[layer, at : at + 8, lanes] * slope
                        drop = jnp.where(valid_at(block + side), drop, 0.0)
                        pair.append(scale * (gpf[layer, at : at + 8, lanes] - drop))
                    at = view * slots + block * 8
                    low = jnp.concatenate(pair, axis=0).astype(BF16)
                    gpb[at : at + 16, lanes] = low
                    gpf[layer, at : at + 16, lanes] = low.astype(F32)

        over_lanes(act)

    def columns_of(slot):
        return pl.ds(pl.multiple_of(slot * own_width, own_width), own_width)

    def place(flips):
        return flips % 2 * 4 + flips // 4 + flips // 2 % 2 * 2

    def grad_copies(layer):
        result = []
        for flips in (7, 6, 5, 4, 3, 2, 1):
            peer, slot = group_peer(flips)
            result.append(
                remote(
                    gpf.at[layer, :, columns_of(slot)],
                    gr.at[layer, place(flips) - 1],
                    sem_g,
                    (layer, flips - 1),
                    peer,
                )
            )
        return result

    def back_project():
        for at in range(0, hidden, tile):
            span = min(tile, hidden - at)
            gy[:, at : at + span] += lax.dot_general(
                gpb[:, :hidden],
                wbuf[at : at + span, :],
                (((1,), (1,)), ((), ())),
                preferred_element_type=F32,
            )

    def load_factors(layer):
        for copy in grad_copies(layer):
            copy.wait_recv()
        gb[0:rows, :] = gpf[layer, :, columns_of(mine)].astype(BF16)
        for at in range(1, 8):
            gb[at * rows : (at + 1) * rows, :] = gr[layer, at - 1].astype(BF16)
        for at in range(4):
            if layer == 1:
                y_copy(at).wait_recv()
            elif at:
                core_copy(at - 1).wait_recv()
            else:
                for k in range(8):
                    x_copy(k, 2).wait_recv()

    def span_of(k):
        start, span = plan[k]
        return slice(start, start + span)

    def weight_product(layer, k):
        if k == 0:
            load_factors(layer)
        start, span = plan[k]
        for at in range(8):
            if layer == 0:
                source = x0f if at == 0 else xs.at[at - 1] if at < 4 else xo.at[at - 4]
            else:
                source = ys.at[at] if at < 4 else yo.at[at - 4]
            xchunk[at * rows : (at + 1) * rows, :span] = source[:, span_of(k)].astype(BF16)
        dw[layer, span_of(k), :] = lax.dot_general(
            xchunk[:, :span], gb[...], (((0,), (0,)), ((), ())), preferred_element_type=F32
        )
        fold_copy(layer, k, 0).start()

    def bit_of(at):
        return a // 2**at % 2

    def bit_peer(at):
        return device(a + (1 - 2 * bit_of(at)) * 2**at, bx, by, c)

    def region(k, count):
        start, span = plan[k]
        first = start
        for at in range(count):
            first = first + bit_of(at) * (span >> (at + 1))
        return first

    def rows_at(first, count):
        return pl.ds(pl.multiple_of(first, 8), count)

    def fold_copy(layer, k, at):
        start, span = plan[k]
        part = span >> (at + 1)
        source = rows_at(region(k, at) + (1 - bit_of(at)) * part, part)
        landing = start + span - (span >> at)
        return remote(
            dw.at[layer, source],
            rb.at[layer, slice(landing, landing + part)],
            sem_rs,
            (layer, k, at),
            bit_peer(at),
        )

    def fold(layer, k, at):
        fold_copy(layer, k, at).wait_recv()
        start, span = plan[k]
        part = span >> (at + 1)
        landing = start + span - (span >> at)
        kept = rows_at(region(k, at + 1), part)
        dw[layer, kept, :] = dw[layer, kept, :] + rb[layer, landing : landing + part, :]
        if at + 1 < bits:
            fold_copy(layer, k, at + 1).start()
        else:
            local_copy(layer, k).start()
            widen_copy(layer, k, at).start()

    def local_copy(layer, k):
        kept = rows_at(region(k, bits), plan[k][1] >> bits)
        return pltpu.make_async_copy(
            dw.at[layer, kept], grad_weights.at[layer, kept, columns_of(mine)], sem_l.at[layer, k]
        )

    def widen_copy(layer, k, at):
        held = rows_at(region(k, at + 1), plan[k][1] >> (at + 1))
        landing = grad_weights.at[layer, held, columns_of(mine)]
        source = dw.at[layer, held] if at + 1 == bits else landing
        return remote(source, landing, sem_az, (layer, k, at), bit_peer(at))

    def widen(layer, k, at):
        part = plan[k][1] >> (at + 1)
        other = rows_at(region(k, at) + (1 - bit_of(at)) * part, part)
        landing = grad_weights.at[layer, other, columns_of(mine)]
        remote(landing, landing, sem_az, (layer, k, at), bit_peer(at)).wait_recv()
        if at + 1 == bits:
            local_copy(layer, k).wait()
        if at:
            widen_copy(layer, k, at - 1).start()
        else:
            for kind in (0, 1, 3):
                block_copy(layer, k, kind).start()

    def order_of(layer, k):
        own, flip_x = (bx, by), (nx, by)
        flip_y, both = (bx, ny), (nx, ny)
        if (k + layer) % 2 == 1:
            return (own, flip_x, flip_y, both), x_peer, y_peer
        return (own, flip_y, flip_x, both), y_peer, x_peer

    def block(layer, k, x_at, y_at, c_at):
        return grad_weights.at[layer, span_of(k), columns_of(x_at * 4 + y_at * 2 + c_at)]

    def block_copy(layer, k, kind):
        spots, first, second = order_of(layer, k)
        spot, peer = {
            0: (0, first),
            1: (0, second),
            2: (1, second),
            3: (0, core_peer),
            4: (1, core_peer),
            5: (2, core_peer),
            6: (3, core_peer),
        }[kind]
        held = block(layer, k, *spots[spot], c)
        return remote(held, held, sem_ag, (layer, k, kind), peer)

    def arrived(layer, k, kind):
        spots, first, second = order_of(layer, k)
        spot = {0: 1, 1: 2, 2: 3, 3: 0, 4: 1, 5: 2, 6: 3}[kind]
        landing = block(layer, k, *spots[spot], nc if kind >= 3 else c)
        remote(landing, landing, sem_ag, (layer, k, kind), core_peer).wait_recv()

    def gather(layer, k, at):
        arrived(layer, k, at)
        if at == 0:
            block_copy(layer, k, 2).start()
        block_copy(layer, k, 4 + at).start()

    def write_out(target, value, at):
        ob[...] = value
        copy = pltpu.make_async_copy(ob, target, sem_io.at[at])
        copy.start()
        return copy

    send_x(0, 1)
    load_weight(0, 0).wait()
    project(xb, normed.at[0])
    load_weight(1, 1).start()
    moments(0)
    start_sum(eight_f.at[0], 0)
    send_x(1, 4)
    cotangent_in.wait()
    gy[:, :hidden] = ob[...].astype(F32)
    middle_sum(eight_f.at[0], ring_f.at[0], 0)
    finish_sum(eight_f.at[0], ring_f.at[0], 0, total_f.at[0])
    forward(0)
    y_copy(0).start()
    xb[...] = ys[0, :, :hidden].astype(BF16)
    load_weight(1, 1).wait()
    project(xb, normed.at[1])
    moments(1)
    start_sum(eight_f.at[1], 1)
    send_x(4, 7)
    middle_sum(eight_f.at[1], ring_f.at[1], 1)
    finish_sum(eight_f.at[1], ring_f.at[1], 1, total_f.at[1])
    forward(1)
    backward_sums(1)
    start_sum(eight_b.at[1], 2)
    send_x(7, 8)
    send_diagonal(0, 2)
    result_out = write_out(output, x1[:, :hidden].astype(BF16), 2)
    middle_sum(eight_b.at[1], ring_b.at[1], 2)
    finish_sum(eight_b.at[1], ring_b.at[1], 2, total_b.at[1])
    backward_drive(1)
    send_diagonal(2, 8)
    for copy in grad_copies(1):
        copy.start()
    back_project()
    load_weight(0, 2).start()
    backward_sums(0)
    start_sum(eight_b.at[0], 3)
    wait_x(0)
    wait_x(1)
    load_weight(0, 2).wait()
    repeat_forward(0)
    repeat_forward(1)
    wait_x(2)
    repeat_forward(2)

    def finish_backward(layer, k):
        finish_sum(eight_b.at[0], ring_b.at[0], 3, total_b.at[0])
        backward_drive(0)
        for copy in grad_copies(0):
            copy.start()

    def finish_input(layer, k):
        back_project()
        result_out.wait()
        write_out(grad_frames, gy[:, :hidden].astype(BF16), 3)

    stages = [(weight_product, 0.0)]
    for at in range(bits):
        stages.append((functools.partial(fold, at=at), LAGS[0] * (at + 1)))
    for at in range(bits):
        stages.append(
            (functools.partial(widen, at=bits - 1 - at), LAGS[0] * bits + LAGS[1] * (at + 1))
        )
    for at in range(3):
        stages.append(
            (functools.partial(gather, at=at), LAGS[0] * bits + LAGS[1] * bits + LAGS[2 + at])
        )
    tasks = [
        (SUM_DUE, 0, 0, 0, lambda layer, k: middle_sum(eight_b.at[0], ring_b.at[0], 3)),
        (DRIVE_DUE, 0, 0, 0, finish_backward),
        (INPUT_DUE, 0, 0, 0, finish_input),
    ]
    for layer in (1, 0):
        for k in range(chunks):
            start, span = plan[k]
            size = span / piece_at
            for at, (stage, lag) in enumerate(stages):
                due = ((1 - layer) * padded + start) / piece_at
                tasks.append(
                    (due + lag * (SHARE + (1 - SHARE) * size), -at, layer, k, stage)
                )
    tasks.sort(key=lambda task: task[:2])
    for _, _, layer, k, stage in tasks:
        stage(layer, k)

    pltpu.make_async_copy(ob, grad_frames, sem_io.at[3]).wait()
    for k in range(8):
        for kind in range(4):
            x_copy(k, kind).wait_send()
    for at in range(3):
        core_copy(at).wait_send()
    for at in range(4):
        y_copy(at).wait_send()
    for layer in (1, 0):
        for copy in grad_copies(layer):
            copy.wait_send()
        for k in range(chunks):
            for at in range(bits):
                fold_copy(layer, k, at).wait_send()
                widen_copy(layer, k, at).wait_send()
            for kind in range(7):
                block_copy(layer, k, kind).wait_send()
            for kind in range(3, 7):
                arrived(layer, k, kind)
    for at, eight, around in (
        (0, eight_f.at[0], ring_f.at[0]),
        (1, eight_f.at[1], ring_f.at[1]),
        (2, eight_b.at[1], ring_b.at[1]),
        (3, eight_b.at[0], ring_b.at[0]),
    ):
        for flips in range(1, 8):
            peer, _ = group_peer(flips)
            remote(eight.at[mine], eight.at[mine], sem_e, (at, flips - 1), peer).wait_send()
        for level in range(len(levels)):
            _, own, _ = ring_peer(level, 1)
            each_ring(level, lambda step: ring_copy(around, at, level, step, own).wait_send())


def body(ring, frames, weights, norm_gain, norm_shift, decays, lengths, cotangent):
    _, views, slots, hidden = frames.shape
    width = round_up(hidden, 4 * LANES)
    rows = views * slots
    step_rows = max(width // STEPS, 8 * ring)
    own_width = width // 8
    plan, padded = chunk_plan(hidden, ring, step_rows)
    chunks = len(plan)
    dims = (ring, plan, padded, step_rows, views, slots, hidden, width)
    bits = ring.bit_length() - 1
    around = sum(size for _, size, _ in ring_levels(ring))
    vmem = pl.BlockSpec(memory_space=pltpu.VMEM)
    anywhere = pl.BlockSpec(memory_space=pl.ANY)
    scratch = [
        pltpu.VMEM((hidden, hidden), BF16),
        pltpu.VMEM((rows, width), F32),
        pltpu.VMEM((rows, hidden), BF16),
        pltpu.VMEM((rows, hidden), BF16),
        pltpu.VMEM((3, rows, width), F32),
        pltpu.VMEM((4, rows, width), F32),
        pltpu.VMEM((4, rows, width), F32),
        pltpu.VMEM((4, rows, width), F32),
        pltpu.VMEM((2, rows, width), F32),
        pltpu.VMEM((2, rows, width), F32),
        pltpu.VMEM((rows, width), F32),
        pltpu.VMEM((2, rows, width), F32),
        pltpu.VMEM((rows, width), BF16),
        pltpu.VMEM((2, 7, rows, own_width), F32),
        pltpu.VMEM((8 * rows, step_rows), BF16),
        pltpu.VMEM((8 * rows, own_width), BF16),
        pltpu.VMEM((2, padded, own_width), F32),
        pltpu.VMEM((2, padded, own_width), F32),
        pltpu.VMEM((8, width), F32),
        pltpu.VMEM((2, width), F32),
        pltpu.VMEM((2, 8, 2, width), F32),
        pltpu.VMEM((2, 8, 4, width), F32),
        pltpu.VMEM((2, around, 2, width), F32),
        pltpu.VMEM((2, around, 4, width), F32),
        pltpu.VMEM((2, 2, width), F32),
        pltpu.VMEM((2, 4, width), F32),
        pltpu.SemaphoreType.DMA((3,)),
        pltpu.SemaphoreType.DMA((4,)),
        pltpu.SemaphoreType.DMA((2, 8, 4)),
        pltpu.SemaphoreType.DMA((2, 3)),
        pltpu.SemaphoreType.DMA((2, 4)),
        pltpu.SemaphoreType.DMA((2, 2, 7)),
        pltpu.SemaphoreType.DMA((2, 4, 7)),
        pltpu.SemaphoreType.DMA((2, 4, around)),
        pltpu.SemaphoreType.DMA((2, 2, chunks, bits)),
        pltpu.SemaphoreType.DMA((2, 2, chunks, bits)),
        pltpu.SemaphoreType.DMA((2, 2, chunks, 7)),
        pltpu.SemaphoreType.DMA((2, chunks)),
    ]
    small = jax.ShapeDtypeStruct((2, hidden), F32)
    flat = jax.ShapeDtypeStruct((rows, hidden), BF16)
    result, grad_first, grad_weights, grad_gain, grad_shift, grad_decay = pl.pallas_call(
        functools.partial(kernel, dims),
        out_shape=(
            flat,
            flat,
            jax.ShapeDtypeStruct((2, padded, width), F32),
            small,
            small,
            small,
        ),
        in_specs=[
            anywhere,
            anywhere,
            vmem,
            vmem,
            vmem,
            pl.BlockSpec(memory_space=pltpu.SMEM),
            anywhere,
        ],
        out_specs=(anywhere, anywhere, anywhere, vmem, vmem, vmem),
        scratch_shapes=scratch,
        compiler_params=pltpu.CompilerParams(
            collective_id=0, has_side_effects=True, vmem_limit_bytes=60 << 20
        ),
    )(
        frames.reshape(rows, hidden),
        weights,
        norm_gain,
        norm_shift,
        decays,
        lengths,
        cotangent.reshape(rows, hidden),
    )
    grad_weights = grad_weights[:, :hidden, :hidden]
    return (
        result.reshape(frames.shape),
        grad_first.reshape(frames.shape),
        grad_weights,
        grad_gain,
        grad_shift,
        grad_decay,
    )


def solution(mesh):
    everywhere = P(("dp", "rep"), None, None, None)
    return jax.shard_map(
        functools.partial(body, mesh.shape["dp"] // 2),
        mesh=mesh,
        in_specs=(everywhere, P(), P(), P(), P(), P(("dp", "rep")), everywhere),
        out_specs=(everywhere, everywhere, P(), P(), P(), P()),
        check_vma=False,
    )
```

```python
import functools

import jax
import jax.numpy as jnp
from jax import lax
from jax.experimental import pallas as pl
from jax.experimental.pallas import tpu as pltpu
from jax.sharding import PartitionSpec as P

EPS = 1e-05
MESH = pl.DeviceIdType.MESH
F32 = jnp.float32
BF16 = jnp.bfloat16
LAGS = (1.06, 0.71, 1.63, 1.73, 4.42)
SUM_DUE = 0.43
DRIVE_DUE = 1.4
INPUT_DUE = 2.4
SHARE = 0.72
STEPS = 16
LANES = 128


def round_up(value, unit):
    return -(-value // unit) * unit


def chunk_plan(hidden, ring, step):
    plan, start = [], 0
    while start < hidden:
        span = min(step, round_up(hidden - start, 8 * ring))
        plan.append((start, span))
        start += span
    return tuple(plan), start


def ring_levels(ring):
    inner = min(4, ring)
    levels = [(1, inner, 0)]
    if ring > inner:
        levels.append((inner, ring // inner, inner))
    return tuple(levels)


def kernel(
    dims,
    frames,
    weights,
    gain,
    shift,
    decay,
    lengths,
    cotangent,
    output,
    grad_frames,
    grad_weights,
    grad_gain,
    grad_shift,
    grad_decay,
    wbuf,
    x0f,
    xb,
    ob,
    xs,
    xo,
    ys,
    yo,
    normed,
    states,
    gy,
    gpf,
    gpb,
    gr,
    xchunk,
    gb,
    dw,
    rb,
    params,
    coef,
    eight_f,
    eight_b,
    ring_f,
    ring_b,
    total_f,
    total_b,
    sem_w,
    sem_io,
    sem_x,
    sem_c,
    sem_y,
    sem_g,
    sem_e,
    sem_r,
    sem_rs,
    sem_az,
    sem_ag,
    sem_l,
):
    ring, plan, padded, _, views, slots, hidden, width = dims
    chunks = len(plan)
    rows = views * slots
    piece_at = width // 8
    own_width = width // 8
    levels = ring_levels(ring)
    x1 = gpf.at[0]
    bits = ring.bit_length() - 1
    tile = 512
    blocks = slots // 8
    lane_steps = width // LANES

    dp, rep = lax.axis_index("dp"), lax.axis_index("rep")
    a, bx = dp // 2, dp % 2
    by, c = rep // 2, rep % 2
    nx, ny, nc = 1 - bx, 1 - by, 1 - c

    def device(a_at, x_at, y_at, c_at):
        return (a_at * 2 + x_at, y_at * 2 + c_at)

    core_peer = device(a, bx, by, nc)
    x_peer = device(a, nx, by, c)
    y_peer = device(a, bx, ny, c)

    def group_peer(flips):
        fx, fy, fc = flips // 4, flips // 2 % 2, flips % 2
        x_at, y_at, c_at = (nx if fx else bx), (ny if fy else by), (nc if fc else c)
        return device(a, x_at, y_at, c_at), x_at * 4 + y_at * 2 + c_at

    def ring_peer(level, step):
        stride, size, _ = levels[level]
        at = a // stride % size
        to = lax.rem(at + step, size)
        return device(a + (to - at) * stride, bx, by, c), at, to

    def each_ring(level, act):
        for step in range(1, levels[level][1]):
            act(step)

    def remote(src, dst, sems, at, target):
        return pltpu.make_async_remote_copy(
            src_ref=src,
            dst_ref=dst,
            send_sem=sems.at[(0,) + at],
            recv_sem=sems.at[(1,) + at],
            device_id=target,
            device_id_type=MESH,
        )

    barrier = pltpu.get_barrier_semaphore()
    for flips in range(1, 8):
        pl.semaphore_signal(barrier, 1, device_id=group_peer(flips)[0], device_id_type=MESH)
    for level in range(len(levels)):
        each_ring(
            level,
            lambda step: pl.semaphore_signal(
                barrier, 1, device_id=ring_peer(level, step)[0], device_id_type=MESH
            ),
        )

    def load_weight(layer, at):
        return pltpu.make_async_copy(weights.at[layer], wbuf, sem_w.at[at])

    frames_in = pltpu.make_async_copy(frames, xb, sem_io.at[0])
    frames_in.start()
    load_weight(0, 0).start()
    cotangent_in = pltpu.make_async_copy(cotangent, ob, sem_io.at[1])
    cotangent_in.start()

    length = lengths[0]
    tail = hidden - hidden % LANES
    x0f[:, tail:width] = jnp.broadcast_to(length.astype(F32), (rows, width - tail))
    gy[:, tail:width] = jnp.zeros((rows, width - tail), F32)
    frames_in.wait()
    x0f[:, :hidden] = xb[...].astype(F32)
    params[...] = jnp.zeros(params.shape, F32)
    for at, source in enumerate((gain, shift, decay)):
        params[at * 2 : at * 2 + 2, :hidden] = source[...]
    pl.semaphore_wait(barrier, 7 + sum(size - 1 for _, size, _ in levels))

    def piece(k):
        return slice(k * piece_at, (k + 1) * piece_at)

    def x_copy(k, kind):
        if kind == 3:
            source, target = (xs.at[0], y_peer) if k % 2 == 0 else (xs.at[1], x_peer)
            landing = xs.at[2]
        else:
            source = x0f
            landing, target = ((xs.at[0], x_peer), (xs.at[1], y_peer), (xo.at[0], core_peer))[kind]
        return remote(source.at[:, piece(k)], landing.at[:, piece(k)], sem_x, (k, kind), target)

    def send_x(first, last):
        for k in range(first, last):
            for kind in range(3):
                x_copy(k, kind).start()

    def send_diagonal(first, last):
        for k in range(first, last):
            x_copy(k, k % 2).wait_recv()
            x_copy(k, 3).start()

    def core_copy(at):
        return remote(xs.at[at], xo.at[at + 1], sem_c, (at,), core_peer)

    def wait_x(at):
        for k in range(8):
            if at == 2:
                x_copy(k, 3).wait_recv()
            elif k % 2 != at:
                x_copy(k, at).wait_recv()
        core_copy(at).start()

    def y_copy(at):
        return remote(ys.at[at], yo.at[at], sem_y, (at,), core_peer)

    row_at = lax.broadcasted_iota(jnp.int32, (8, LANES), 0)
    def lanes_of(step):
        return pl.ds(pl.multiple_of(step * LANES, LANES), LANES)

    def over_lanes(act):
        def go(step, _):
            act(lanes_of(step), step)
            return 0

        lax.fori_loop(0, lane_steps, go, 0)

    def valid_at(block, limit=None):
        return (row_at + block * 8).astype(F32) < (length.astype(F32) if limit is None else limit)

    def spread(row):
        return jnp.broadcast_to(row, (8, LANES))

    def row_powers(decay_row, reverse):
        one = spread(decay_row)
        two = one * one
        four = two * two
        from_edge = 7 - row_at if reverse else row_at
        ones = jnp.ones((8, LANES), F32)
        power = (
            one
            * jnp.where(from_edge % 2 == 1, one, ones)
            * jnp.where(from_edge // 2 % 2 == 1, two, ones)
            * jnp.where(from_edge // 4 == 1, four, ones)
        )
        zero = jnp.zeros((8, LANES), F32)
        return (
            jnp.where(from_edge >= 1, one, zero),
            jnp.where(from_edge >= 2, two, zero),
            jnp.where(from_edge >= 4, four, zero),
            power,
        )

    def scan_blocks(values, powers, reverse):
        one, two, four, power = powers
        count = len(values)
        order = range(count - 1, -1, -1) if reverse else range(count)
        result = [None] * count
        carry = None
        for at in order:
            value = values[at]
            for amount, factor in ((1, one), (2, two), (4, four)):
                value = value + factor * pltpu.roll(value, 8 - amount if reverse else amount, 0)
            if carry is not None:
                value = value + power * carry
            carry = spread(value[0:1] if reverse else value[7:8])
            result[at] = value
        return result

    def project(source, result):
        for at in range(0, hidden, tile):
            span = min(tile, hidden - at)
            result[:, at : at + span] = jnp.dot(
                source[...], wbuf[:, at : at + span], preferred_element_type=F32
            )
        if tail < hidden:
            kept = result[:, tail:width]
            lane = lax.broadcasted_iota(jnp.int32, kept.shape, 1)
            result[:, tail:width] = jnp.where(lane < hidden - tail, kept, 0.0)

    mine = bx * 4 + by * 2 + c

    def moments(layer):
        frame_count = (views * length).astype(F32)

        def act(lanes, step):
            first = jnp.zeros((8, LANES), F32)
            square = jnp.zeros((8, LANES), F32)
            for view in range(views):
                for block in range(blocks):
                    value = normed[layer, view * slots + block * 8 : view * slots + block * 8 + 8, lanes]
                    value = jnp.where(valid_at(block), value, 0.0)
                    first += value
                    square += value * value
            first = jnp.sum(first, axis=0, keepdims=True)
            lane = lax.broadcasted_iota(jnp.int32, (1, LANES), 1) + step * LANES
            first = jnp.where(lane >= hidden, frame_count, first)
            eight_f[layer, mine, 0:1, lanes] = first
            eight_f[layer, mine, 1:2, lanes] = jnp.sum(square, axis=0, keepdims=True)

        over_lanes(act)

    def start_sum(eight, at):
        for flips in range(1, 8):
            peer, _ = group_peer(flips)
            remote(eight.at[mine], eight.at[mine], sem_e, (at, flips - 1), peer).start()

    def ring_copy(around, at, level, step, slot):
        _, _, first = levels[level]
        peer, _, _ = ring_peer(level, step)
        ref = around.at[first + slot]
        return remote(ref, ref, sem_r, (at, first + step), peer)

    def ring_send(around, at, level, total):
        _, _, first = levels[level]
        _, own, _ = ring_peer(level, 1)
        around[first + own] = total
        each_ring(level, lambda step: ring_copy(around, at, level, step, own).start())

    def middle_sum(eight, around, at):
        for flips in range(1, 8):
            peer, slot = group_peer(flips)
            remote(eight.at[mine], eight.at[slot], sem_e, (at, flips - 1), peer).wait_recv()
        total = eight[0]
        for slot in range(1, 8):
            total = total + eight[slot]
        ring_send(around, at, 0, total)

    def finish_sum(eight, around, at, result):
        for level, (stride, size, first) in enumerate(levels):

            def wait(step):
                behind = lax.rem(a // stride % size + size - step, size)
                ring_copy(around, at, level, step, behind).wait_recv()

            each_ring(level, wait)
            total = around[first]
            for slot in range(1, size):
                total = total + around[first + slot]
            if level + 1 < len(levels):
                ring_send(around, at, level + 1, total)
        result[...] = total

    def statistics(layer, lanes):
        count = jnp.broadcast_to(total_f[layer, 0:1, width - 1 : width], (1, LANES))
        average = total_f[layer, 0:1, lanes] / count
        variance = total_f[layer, 1:2, lanes] / count - average * average
        return average, lax.rsqrt(variance + EPS), count

    def forward(layer):
        def act(lanes, step):
            average, inverse, _ = statistics(layer, lanes)
            coef[layer : layer + 1, lanes] = inverse
            average, inverse = spread(average), spread(inverse)
            gain_row = spread(params[layer : layer + 1, lanes])
            shift_row = spread(params[2 + layer : 3 + layer, lanes])
            powers = row_powers(params[4 + layer : 5 + layer, lanes], False)
            for view in range(views):
                drives = []
                for block in range(blocks):
                    at = view * slots + block * 8
                    value = (normed[layer, at : at + 8, lanes] - average) * inverse
                    normed[layer, at : at + 8, lanes] = value
                    drives.append(gain_row * value + shift_row)
                result = scan_blocks(drives, powers, False)
                for block in range(blocks):
                    at = view * slots + block * 8
                    state = result[block]
                    states[layer, at : at + 8, lanes] = state
                    bump = jnp.where(valid_at(block), softplus(state), 0.0)
                    if layer == 0:
                        following = x0f[at : at + 8, lanes] + bump
                        x1[at : at + 8, lanes] = following
                        ys[0, at : at + 8, lanes] = following.astype(BF16).astype(F32)
                    else:
                        x1[at : at + 8, lanes] = x1[at : at + 8, lanes] + bump

        over_lanes(act)

    def softplus(state):
        return jnp.maximum(state, 0.0) + jnp.log1p(jnp.exp(-jnp.abs(state)))

    def repeat_forward(at):
        xb[...] = xs[at, :, :hidden].astype(BF16)
        project(xb, ys.at[at + 1])
        limit = spread(xs[at, 0:1, width - LANES : width])
        limit = jnp.broadcast_to(limit[:, LANES - 1 :], (8, LANES))

        def act(lanes, step):
            average, inverse, _ = statistics(0, lanes)
            gain_row = spread(params[0:1, lanes] * inverse)
            shift_row = spread(params[2:3, lanes] - average * inverse * params[0:1, lanes])
            powers = row_powers(params[4:5, lanes], False)
            for view in range(views):
                drives = []
                for block in range(blocks):
                    row = view * slots + block * 8
                    drives.append(gain_row * ys[at + 1, row : row + 8, lanes] + shift_row)
                result = scan_blocks(drives, powers, False)
                for block in range(blocks):
                    row = view * slots + block * 8
                    bump = jnp.where(valid_at(block, limit), softplus(result[block]), 0.0)
                    following = xs[at, row : row + 8, lanes] + bump
                    ys[at + 1, row : row + 8, lanes] = following.astype(BF16).astype(F32)

        over_lanes(act)
        y_copy(at + 1).start()

    def backward_sums(layer):
        def act(lanes, step):
            powers = row_powers(params[4 + layer : 5 + layer, lanes], True)
            sums = [jnp.zeros((8, LANES), F32) for _ in range(3)]
            for view in range(views):
                sources = []
                kept = []
                for block in range(blocks):
                    at = view * slots + block * 8
                    state = states[layer, at : at + 8, lanes]
                    kept.append(state)
                    slope = 1.0 / (1.0 + jnp.exp(-state))
                    slope = gy[at : at + 8, lanes] * slope
                    sources.append(jnp.where(valid_at(block), slope, 0.0))
                carried = scan_blocks(sources, powers, True)
                for block in range(blocks):
                    at = view * slots + block * 8
                    value = carried[block]
                    gpf[layer, at : at + 8, lanes] = value
                    shifted = pltpu.roll(kept[block], 1, 0)
                    before = spread(kept[block - 1][7:8]) if block else jnp.zeros((8, LANES), F32)
                    shifted = jnp.where(row_at == 0, before, shifted)
                    sums[0] += value * normed[layer, at : at + 8, lanes]
                    sums[1] += value
                    sums[2] += value * shifted
            for at in range(3):
                eight_b[layer, mine, at : at + 1, lanes] = jnp.sum(sums[at], axis=0, keepdims=True)
            eight_b[layer, mine, 3:4, lanes] = jnp.zeros((1, LANES), F32)

        over_lanes(act)

    def backward_drive(layer):
        grad_gain[layer : layer + 1, :] = total_b[layer, 0:1, :hidden]
        grad_shift[layer : layer + 1, :] = total_b[layer, 1:2, :hidden]
        grad_decay[layer : layer + 1, :] = total_b[layer, 2:3, :hidden]

        def act(lanes, step):
            count = jnp.broadcast_to(total_f[layer, 0:1, width - 1 : width], (1, LANES))
            slope = spread(total_b[layer, 0:1, lanes] / count)
            offset = spread(total_b[layer, 1:2, lanes] / count)
            scale = spread(coef[layer : layer + 1, lanes] * params[layer : layer + 1, lanes])
            for view in range(views):
                for block in range(0, blocks, 2):
                    pair = []
                    for side in range(2):
                        at = view * slots + (block + side) * 8
                        drop = offset + normed[layer, at : at + 8, lanes] * slope
                        drop = jnp.where(valid_at(block + side), drop, 0.0)
                        pair.append(scale * (gpf[layer, at : at + 8, lanes] - drop))
                    at = view * slots + block * 8
                    low = jnp.concatenate(pair, axis=0).astype(BF16)
                    gpb[at : at + 16, lanes] = low
                    gpf[layer, at : at + 16, lanes] = low.astype(F32)

        over_lanes(act)

    def columns_of(slot):
        return pl.ds(pl.multiple_of(slot * own_width, own_width), own_width)

    def place(flips):
        return flips % 2 * 4 + flips // 4 + flips // 2 % 2 * 2

    def grad_copies(layer):
        result = []
        for flips in (7, 6, 5, 4, 3, 2, 1):
            peer, slot = group_peer(flips)
            result.append(
                remote(
                    gpf.at[layer, :, columns_of(slot)],
                    gr.at[layer, place(flips) - 1],
                    sem_g,
                    (layer, flips - 1),
                    peer,
                )
            )
        return result

    def back_project():
        for at in range(0, hidden, tile):
            span = min(tile, hidden - at)
            gy[:, at : at + span] += lax.dot_general(
                gpb[:, :hidden],
                wbuf[at : at + span, :],
                (((1,), (1,)), ((), ())),
                preferred_element_type=F32,
            )

    def load_factors(layer):
        for copy in grad_copies(layer):
            copy.wait_recv()
        gb[0:rows, :] = gpf[layer, :, columns_of(mine)].astype(BF16)
        for at in range(1, 8):
            gb[at * rows : (at + 1) * rows, :] = gr[layer, at - 1].astype(BF16)
        for at in range(4):
            if layer == 1:
                y_copy(at).wait_recv()
            elif at:
                core_copy(at - 1).wait_recv()
            else:
                for k in range(8):
                    x_copy(k, 2).wait_recv()

    def span_of(k):
        start, span = plan[k]
        return slice(start, start + span)

    def weight_product(layer, k):
        if k == 0:
            load_factors(layer)
        start, span = plan[k]
        for at in range(8):
            if layer == 0:
                source = x0f if at == 0 else xs.at[at - 1] if at < 4 else xo.at[at - 4]
            else:
                source = ys.at[at] if at < 4 else yo.at[at - 4]
            xchunk[at * rows : (at + 1) * rows, :span] = source[:, span_of(k)].astype(BF16)
        dw[layer, span_of(k), :] = lax.dot_general(
            xchunk[:, :span], gb[...], (((0,), (0,)), ((), ())), preferred_element_type=F32
        )
        fold_copy(layer, k, 0).start()

    def bit_of(at):
        return a // 2**at % 2

    def bit_peer(at):
        return device(a + (1 - 2 * bit_of(at)) * 2**at, bx, by, c)

    def region(k, count):
        start, span = plan[k]
        first = start
        for at in range(count):
            first = first + bit_of(at) * (span >> (at + 1))
        return first

    def rows_at(first, count):
        return pl.ds(pl.multiple_of(first, 8), count)

    def fold_copy(layer, k, at):
        start, span = plan[k]
        part = span >> (at + 1)
        source = rows_at(region(k, at) + (1 - bit_of(at)) * part, part)
        landing = start + span - (span >> at)
        return remote(
            dw.at[layer, source],
            rb.at[layer, slice(landing, landing + part)],
            sem_rs,
            (layer, k, at),
            bit_peer(at),
        )

    def fold(layer, k, at):
        fold_copy(layer, k, at).wait_recv()
        start, span = plan[k]
        part = span >> (at + 1)
        landing = start + span - (span >> at)
        kept = rows_at(region(k, at + 1), part)
        dw[layer, kept, :] = dw[layer, kept, :] + rb[layer, landing : landing + part, :]
        if at + 1 < bits:
            fold_copy(layer, k, at + 1).start()
        else:
            local_copy(layer, k).start()
            widen_copy(layer, k, at).start()

    def local_copy(layer, k):
        kept = rows_at(region(k, bits), plan[k][1] >> bits)
        return pltpu.make_async_copy(
            dw.at[layer, kept], grad_weights.at[layer, kept, columns_of(mine)], sem_l.at[layer, k]
        )

    def widen_copy(layer, k, at):
        held = rows_at(region(k, at + 1), plan[k][1] >> (at + 1))
        landing = grad_weights.at[layer, held, columns_of(mine)]
        source = dw.at[layer, held] if at + 1 == bits else landing
        return remote(source, landing, sem_az, (layer, k, at), bit_peer(at))

    def widen(layer, k, at):
        part = plan[k][1] >> (at + 1)
        other = rows_at(region(k, at) + (1 - bit_of(at)) * part, part)
        landing = grad_weights.at[layer, other, columns_of(mine)]
        remote(landing, landing, sem_az, (layer, k, at), bit_peer(at)).wait_recv()
        if at + 1 == bits:
            local_copy(layer, k).wait()
        if at:
            widen_copy(layer, k, at - 1).start()
        else:
            for kind in (0, 1, 3):
                block_copy(layer, k, kind).start()

    def order_of(layer, k):
        own, flip_x = (bx, by), (nx, by)
        flip_y, both = (bx, ny), (nx, ny)
        if (k + layer) % 2 == 1:
            return (own, flip_x, flip_y, both), x_peer, y_peer
        return (own, flip_y, flip_x, both), y_peer, x_peer

    def block(layer, k, x_at, y_at, c_at):
        return grad_weights.at[layer, span_of(k), columns_of(x_at * 4 + y_at * 2 + c_at)]

    def block_copy(layer, k, kind):
        spots, first, second = order_of(layer, k)
        spot, peer = {
            0: (0, first),
            1: (0, second),
            2: (1, second),
            3: (0, core_peer),
            4: (1, core_peer),
            5: (2, core_peer),
            6: (3, core_peer),
        }[kind]
        held = block(layer, k, *spots[spot], c)
        return remote(held, held, sem_ag, (layer, k, kind), peer)

    def arrived(layer, k, kind):
        spots, first, second = order_of(layer, k)
        spot = {0: 1, 1: 2, 2: 3, 3: 0, 4: 1, 5: 2, 6: 3}[kind]
        landing = block(layer, k, *spots[spot], nc if kind >= 3 else c)
        remote(landing, landing, sem_ag, (layer, k, kind), core_peer).wait_recv()

    def gather(layer, k, at):
        arrived(layer, k, at)
        if at == 0:
            block_copy(layer, k, 2).start()
        block_copy(layer, k, 4 + at).start()

    def write_out(target, value, at):
        ob[...] = value
        copy = pltpu.make_async_copy(ob, target, sem_io.at[at])
        copy.start()
        return copy

    send_x(0, 1)
    load_weight(0, 0).wait()
    project(xb, normed.at[0])
    load_weight(1, 1).start()
    moments(0)
    start_sum(eight_f.at[0], 0)
    send_x(1, 4)
    cotangent_in.wait()
    gy[:, :hidden] = ob[...].astype(F32)
    middle_sum(eight_f.at[0], ring_f.at[0], 0)
    finish_sum(eight_f.at[0], ring_f.at[0], 0, total_f.at[0])
    forward(0)
    y_copy(0).start()
    xb[...] = ys[0, :, :hidden].astype(BF16)
    load_weight(1, 1).wait()
    project(xb, normed.at[1])
    moments(1)
    start_sum(eight_f.at[1], 1)
    send_x(4, 7)
    middle_sum(eight_f.at[1], ring_f.at[1], 1)
    finish_sum(eight_f.at[1], ring_f.at[1], 1, total_f.at[1])
    forward(1)
    backward_sums(1)
    start_sum(eight_b.at[1], 2)
    send_x(7, 8)
    send_diagonal(0, 2)
    result_out = write_out(output, x1[:, :hidden].astype(BF16), 2)
    middle_sum(eight_b.at[1], ring_b.at[1], 2)
    finish_sum(eight_b.at[1], ring_b.at[1], 2, total_b.at[1])
    backward_drive(1)
    send_diagonal(2, 8)
    for copy in grad_copies(1):
        copy.start()
    back_project()
    load_weight(0, 2).start()
    backward_sums(0)
    start_sum(eight_b.at[0], 3)
    wait_x(0)
    wait_x(1)
    load_weight(0, 2).wait()
    repeat_forward(0)
    repeat_forward(1)
    wait_x(2)
    repeat_forward(2)

    def finish_backward(layer, k):
        finish_sum(eight_b.at[0], ring_b.at[0], 3, total_b.at[0])
        backward_drive(0)
        for copy in grad_copies(0):
            copy.start()

    def finish_input(layer, k):
        back_project()
        result_out.wait()
        write_out(grad_frames, gy[:, :hidden].astype(BF16), 3)

    stages = [(weight_product, 0.0)]
    for at in range(bits):
        stages.append((functools.partial(fold, at=at), LAGS[0] * (at + 1)))
    for at in range(bits):
        stages.append(
            (functools.partial(widen, at=bits - 1 - at), LAGS[0] * bits + LAGS[1] * (at + 1))
        )
    for at in range(3):
        stages.append(
            (functools.partial(gather, at=at), LAGS[0] * bits + LAGS[1] * bits + LAGS[2 + at])
        )
    tasks = [
        (SUM_DUE, 0, 0, 0, lambda layer, k: middle_sum(eight_b.at[0], ring_b.at[0], 3)),
        (DRIVE_DUE, 0, 0, 0, finish_backward),
        (INPUT_DUE, 0, 0, 0, finish_input),
    ]
    for layer in (1, 0):
        for k in range(chunks):
            start, span = plan[k]
            size = span / piece_at
            for at, (stage, lag) in enumerate(stages):
                due = ((1 - layer) * padded + start) / piece_at
                tasks.append(
                    (due + lag * (SHARE + (1 - SHARE) * size), -at, layer, k, stage)
                )
    tasks.sort(key=lambda task: task[:2])
    for _, _, layer, k, stage in tasks:
        stage(layer, k)

    pltpu.make_async_copy(ob, grad_frames, sem_io.at[3]).wait()
    for k in range(8):
        for kind in range(4):
            x_copy(k, kind).wait_send()
    for at in range(3):
        core_copy(at).wait_send()
    for at in range(4):
        y_copy(at).wait_send()
    for layer in (1, 0):
        for copy in grad_copies(layer):
            copy.wait_send()
        for k in range(chunks):
            for at in range(bits):
                fold_copy(layer, k, at).wait_send()
                widen_copy(layer, k, at).wait_send()
            for kind in range(7):
                block_copy(layer, k, kind).wait_send()
            for kind in range(3, 7):
                arrived(layer, k, kind)
    for at, eight, around in (
        (0, eight_f.at[0], ring_f.at[0]),
        (1, eight_f.at[1], ring_f.at[1]),
        (2, eight_b.at[1], ring_b.at[1]),
        (3, eight_b.at[0], ring_b.at[0]),
    ):
        for flips in range(1, 8):
            peer, _ = group_peer(flips)
            remote(eight.at[mine], eight.at[mine], sem_e, (at, flips - 1), peer).wait_send()
        for level in range(len(levels)):
            _, own, _ = ring_peer(level, 1)
            each_ring(level, lambda step: ring_copy(around, at, level, step, own).wait_send())


def settle_kernel(source, result):
    result[...] = source[:, :, : result.shape[2]]


def settle(padded, hidden):
    layers, _, width = padded.shape
    step = hidden // 2 if hidden % 16 == 0 else hidden
    return pl.pallas_call(
        settle_kernel,
        grid=(layers, hidden // step),
        in_specs=[pl.BlockSpec((1, step, width), lambda layer, at: (layer, at, 0))],
        out_specs=pl.BlockSpec((1, step, hidden), lambda layer, at: (layer, at, 0)),
        out_shape=jax.ShapeDtypeStruct((layers, hidden, hidden), padded.dtype),
        compiler_params=pltpu.CompilerParams(vmem_limit_bytes=48 << 20),
    )(padded)


def body(ring, frames, weights, norm_gain, norm_shift, decays, lengths, cotangent):
    _, views, slots, hidden = frames.shape
    width = round_up(hidden, 4 * LANES)
    rows = views * slots
    step_rows = max(width // STEPS, 8 * ring)
    own_width = width // 8
    plan, padded = chunk_plan(hidden, ring, step_rows)
    chunks = len(plan)
    dims = (ring, plan, padded, step_rows, views, slots, hidden, width)
    bits = ring.bit_length() - 1
    around = sum(size for _, size, _ in ring_levels(ring))
    vmem = pl.BlockSpec(memory_space=pltpu.VMEM)
    anywhere = pl.BlockSpec(memory_space=pl.ANY)
    scratch = [
        pltpu.VMEM((hidden, hidden), BF16),
        pltpu.VMEM((rows, width), F32),
        pltpu.VMEM((rows, hidden), BF16),
        pltpu.VMEM((rows, hidden), BF16),
        pltpu.VMEM((3, rows, width), F32),
        pltpu.VMEM((4, rows, width), F32),
        pltpu.VMEM((4, rows, width), F32),
        pltpu.VMEM((4, rows, width), F32),
        pltpu.VMEM((2, rows, width), F32),
        pltpu.VMEM((2, rows, width), F32),
        pltpu.VMEM((rows, width), F32),
        pltpu.VMEM((2, rows, width), F32),
        pltpu.VMEM((rows, width), BF16),
        pltpu.VMEM((2, 7, rows, own_width), F32),
        pltpu.VMEM((8 * rows, step_rows), BF16),
        pltpu.VMEM((8 * rows, own_width), BF16),
        pltpu.VMEM((2, padded, own_width), F32),
        pltpu.VMEM((2, padded, own_width), F32),
        pltpu.VMEM((8, width), F32),
        pltpu.VMEM((2, width), F32),
        pltpu.VMEM((2, 8, 2, width), F32),
        pltpu.VMEM((2, 8, 4, width), F32),
        pltpu.VMEM((2, around, 2, width), F32),
        pltpu.VMEM((2, around, 4, width), F32),
        pltpu.VMEM((2, 2, width), F32),
        pltpu.VMEM((2, 4, width), F32),
        pltpu.SemaphoreType.DMA((3,)),
        pltpu.SemaphoreType.DMA((4,)),
        pltpu.SemaphoreType.DMA((2, 8, 4)),
        pltpu.SemaphoreType.DMA((2, 3)),
        pltpu.SemaphoreType.DMA((2, 4)),
        pltpu.SemaphoreType.DMA((2, 2, 7)),
        pltpu.SemaphoreType.DMA((2, 4, 7)),
        pltpu.SemaphoreType.DMA((2, 4, around)),
        pltpu.SemaphoreType.DMA((2, 2, chunks, bits)),
        pltpu.SemaphoreType.DMA((2, 2, chunks, bits)),
        pltpu.SemaphoreType.DMA((2, 2, chunks, 7)),
        pltpu.SemaphoreType.DMA((2, chunks)),
    ]
    small = jax.ShapeDtypeStruct((2, hidden), F32)
    flat = jax.ShapeDtypeStruct((rows, hidden), BF16)
    result, grad_first, grad_weights, grad_gain, grad_shift, grad_decay = pl.pallas_call(
        functools.partial(kernel, dims),
        out_shape=(
            flat,
            flat,
            jax.ShapeDtypeStruct((2, padded, width), F32),
            small,
            small,
            small,
        ),
        in_specs=[
            anywhere,
            anywhere,
            vmem,
            vmem,
            vmem,
            pl.BlockSpec(memory_space=pltpu.SMEM),
            anywhere,
        ],
        out_specs=(anywhere, anywhere, anywhere, vmem, vmem, vmem),
        scratch_shapes=scratch,
        compiler_params=pltpu.CompilerParams(
            collective_id=0, has_side_effects=True, vmem_limit_bytes=60 << 20
        ),
    )(
        frames.reshape(rows, hidden),
        weights,
        norm_gain,
        norm_shift,
        decays,
        lengths,
        cotangent.reshape(rows, hidden),
    )
    grad_weights = settle(grad_weights, hidden)
    return (
        result.reshape(frames.shape),
        grad_first.reshape(frames.shape),
        grad_weights,
        grad_gain,
        grad_shift,
        grad_decay,
    )


def solution(mesh):
    everywhere = P(("dp", "rep"), None, None, None)
    return jax.shard_map(
        functools.partial(body, mesh.shape["dp"] // 2),
        mesh=mesh,
        in_specs=(everywhere, P(), P(), P(), P(), P(("dp", "rep")), everywhere),
        out_specs=(everywhere, everywhere, P(), P(), P(), P()),
        check_vma=False,
    )
```
